512 devices in a mesh: dp: 32 (over z, y_hi, core), tensor: 4 (over y_lo), replica: 4 (over x).
Axes of the slice: x: 4, y: 8 (y_hi: 2, y_lo: 4; y = y_hi * 4 + y_lo), z: 8, core: 2. Of those that a mesh axis runs over, the one named last changes fastest.
Arguments:
- acts: bfloat16 [32768, 5120], P(('dp', 'replica'), 'tensor'), may hold values from -64 to 64
- out_grads: bfloat16 [32768, 5120], P(('dp', 'replica'), 'tensor'), may hold values from -64 to 64
- grad_parts: bfloat16 [4, 5120, 5120], P('replica', 'dp', 'tensor'), may hold values from -24 to 24
- basis_a: bfloat16 [40, 128, 128], P('tensor'), may hold values from -0.5 to 0.5
- basis_g: bfloat16 [40, 128, 128], P('tensor'), may hold values from -0.5 to 0.5
- fac_old: float32 [4, 32, 128, 128], P('tensor', 'dp'), as said below
- owner_slot: int32 [4, 20], replicated, may hold values from 0 to 31, as said below
Outputs:
- update: bfloat16 [5120, 5120], P('dp', 'tensor')
- fac_new: float32 [4, 32, 128, 128], P('tensor', 'dp')
The draws below stay inside these ranges and needn't reach their ends.
Inputs may be any that keep to these rules, and one draw needn't show every extreme that they name: `owner_slot`: each row names 20 different slots; slot s belongs to owner s // 1 on dp; in each row some owner holds 1 factors. `fac_old`: each block is symmetric positive definite.
All inputs are finite; a program needn't handle non-finite values.
Results may differ from the reference program's by a relative error of at most 0.019.
Values may be sent and summed in bfloat16 or wider, within the bound.
A program may use at most 64 MiB of HBM per device.

```python
import math
import jax
import jax.numpy as jnp
from jax import lax

D = 5120
BLK = 128
NB = 40
HB = 10
FPT = 20
SLOTS = 1
TOKENS = 32768
N_DP = 32
N_TENSOR = 4
N_REPLICA = 4


def draw_owner_slot(key, part):
    key = jax.random.fold_in(key, 11)
    slot_total = N_DP * SLOTS

    def one_row(row_key):
        first_key, second_key, third_key = jax.random.split(row_key, 3)
        ordering = jax.random.permutation(first_key, slot_total).astype(jnp.int32)
        favored = jax.random.randint(second_key, (), 0, N_DP).astype(jnp.int32)
        owners = jnp.arange(slot_total, dtype=jnp.int32) // SLOTS
        scores = ordering - jnp.where(owners == favored, slot_total, 0).astype(jnp.int32)
        ranked = jnp.argsort(scores, stable=True)[:FPT].astype(jnp.int32)
        return jax.random.permutation(third_key, ranked).astype(jnp.int32)
    return jax.vmap(one_row)(jax.random.split(key, N_TENSOR))


def draw_fac_old(key, part):
    key = jax.random.fold_in(key, 23)
    diag_key, off_key = jax.random.split(key)
    full_shape = (N_TENSOR, N_DP * SLOTS, BLK, BLK)
    diagonal = jnp.exp(jax.random.uniform(diag_key, full_shape[:3], jnp.float32, math.log(2.0), math.log(6.0)))
    off_reach = 1.8 / BLK
    noise_raw = jax.random.uniform(off_key, full_shape, jnp.float32, -off_reach, off_reach)
    symmetric = 0.5 * (noise_raw + jnp.swapaxes(noise_raw, 2, 3))
    identity = jnp.eye(BLK, dtype=jnp.float32)
    return symmetric * (1.0 - identity) + diagonal[..., None] * identity


def with_spikes(entries, key, source, target, blocks, factor):
    owner, partner = [(jnp.arange(entries.shape[position]) // (entries.shape[position] // blocks)).reshape([-1 if axis == position else 1 for axis in range(entries.ndim)]) for position in (source, target)]
    chosen = jax.random.permutation(key, blocks)[partner]
    strong = (owner == chosen) | (owner == (partner + blocks // 2) % blocks)
    return jnp.where(strong, factor * entries, entries)


def block_levels(own_key, shape, cuts, low, top_value):
    loudness = 1.0
    for axis_at, shards_of in cuts:
        heights = jax.random.uniform(jax.random.fold_in(jax.random.fold_in(own_key, 6), axis_at), (shards_of,), jnp.float32, low / len(cuts), top_value / len(cuts))
        loudness = loudness * jnp.repeat(jnp.exp(heights), shape[axis_at] // shards_of).reshape((-1,) + (1,) * (len(shape) - 1 - axis_at))
    return loudness


def noise(key, dims, width, reach, shards=(), kind=jnp.bfloat16):
    entries = width * jax.random.normal(key, dims, jnp.float32)
    if shards:
        entries = entries * block_levels(key, dims, shards, -0.22, 0.18)
    return jnp.clip(entries, -reach, reach).astype(kind)


def noise_with(key, extent, deviation, limit, shards, heavy, kind=jnp.bfloat16):
    array = deviation * jax.random.normal(key, extent, jnp.float32)
    if shards:
        array = array * block_levels(key, extent, shards, -0.22, 0.18)
    return jnp.clip(with_spikes(array, jax.random.fold_in(key, 3), *heavy), -limit, limit).astype(kind)


def setup_inputs(seed: int = 0) -> dict:
    arg_keys = jax.random.split(jax.random.key(seed), 8)
    acts = noise_with(arg_keys[0], (TOKENS, D), 3.0, 64.0, ((0, 128), (1, 4)), (0, 1, 128, 5.5))
    out_grads = noise_with(arg_keys[1], (TOKENS, D), 3.0, 64.0, ((0, 128), (1, 4)), (0, 1, 128, 5.5))
    grad_parts = noise(arg_keys[2], (N_REPLICA, D, D), 4.0, 24.0, ((0, 4), (1, 32), (2, 4)))
    basis_a = noise(arg_keys[3], (NB, BLK, BLK), BLK ** -0.5, 0.5, ((0, 4),))
    basis_g = noise(arg_keys[4], (NB, BLK, BLK), BLK ** -0.5, 0.5, ((0, 4),))
    fac_old = draw_fac_old(jax.random.fold_in(arg_keys[7], 71), 0)
    owner_slot = draw_owner_slot(jax.random.fold_in(arg_keys[7], 71), 0)
    return {"acts": acts, "out_grads": out_grads, "grad_parts": grad_parts, "basis_a": basis_a, "basis_g": basis_g, "fac_old": fac_old, "owner_slot": owner_slot}


decay_rate = 0.5
damping = 0.01


def block_cov(matrix, index):
    piece = lax.dynamic_slice_in_dim(matrix, index * BLK, BLK, 1)
    return jnp.dot(piece.T, piece, preferred_element_type=jnp.float32)


def reference(acts, out_grads, grad_parts, basis_a, basis_g, fac_old, owner_slot):
    block_ids = jnp.arange(NB, dtype=jnp.int32)
    cov_in = lax.map(lambda index: block_cov(acts, index), block_ids) / TOKENS
    cov_out = lax.map(lambda index: block_cov(out_grads, index), block_ids) / TOKENS
    cov_all = jnp.concatenate([cov_in.reshape(N_TENSOR, HB, BLK, BLK), cov_out.reshape(N_TENSOR, HB, BLK, BLK)], 1)
    bases_all = jnp.concatenate([basis_a.reshape(N_TENSOR, HB, BLK, BLK), basis_g.reshape(N_TENSOR, HB, BLK, BLK)], 1).astype(jnp.float32)
    tensor_ids = jnp.arange(N_TENSOR, dtype=jnp.int32)[:, None]
    previous = fac_old[tensor_ids, owner_slot]
    refreshed = decay_rate * previous + (1.0 - decay_rate) * cov_all
    fac_new = fac_old.at[tensor_ids, owner_slot].set(refreshed)
    turned_fac = jnp.einsum("tfij,tfjk->tfik", refreshed, bases_all, precision=lax.Precision.HIGHEST)
    eigen = jnp.sum(bases_all * turned_fac, axis=2)
    eig_in = eigen[:, :HB].reshape(D)
    eig_out = eigen[:, HB:].reshape(D)
    grad = jnp.sum(grad_parts.astype(jnp.float32), axis=0).astype(jnp.bfloat16)
    qa_full = basis_a.astype(jnp.float32)
    qg_full = basis_g.astype(jnp.float32)
    turned = jnp.einsum("rbi,bij->rbj", grad.reshape(D, NB, BLK).astype(jnp.float32), qa_full).reshape(D, D).astype(jnp.bfloat16)
    inner_rot = jnp.einsum("bij,biw->bjw", qg_full, turned.reshape(NB, BLK, D).astype(jnp.float32))
    scaled = (inner_rot / (eig_out.reshape(NB, BLK, 1) * eig_in[None, None, :] + damping)).astype(jnp.bfloat16)
    rotated_back = jnp.einsum("bij,bjw->biw", qg_full, scaled.astype(jnp.float32)).reshape(D, D).astype(jnp.bfloat16)
    update = jnp.einsum("rbj,bij->rbi", rotated_back.reshape(D, NB, BLK).astype(jnp.float32), qa_full).reshape(D, D).astype(jnp.bfloat16)
    return update, fac_new
```

```python
import jax
import jax.numpy as jnp
from jax import lax
from jax.experimental import pallas as pl
from jax.experimental.pallas import tpu as pltpu
from jax.sharding import PartitionSpec as P

MESH = pl.DeviceIdType.MESH
F32, BF16 = jnp.float32, jnp.bfloat16

DECAY = 0.5
DAMPING = 0.01
TOKENS = 32768
BLK = 128
HEADS = 10
FACTORS = 2 * HEADS
ROWS = 160
WIN = 2 * BLK
SLOTS = 32
Z, R = 8, 4


def contract(a, b, da, db):
    return lax.dot_general(a, b, (((da,), (db,)), ((), ())), preferred_element_type=F32)


def kernel(
    owner, acts_hbm, grads_hbm, parts_hbm, qa_hbm, qg_hbm, fac_hbm,
    update_hbm, fac_out,
    acts, outg, part, bases, fac, gwin, cov, slot_f, slot_u,
    v0_send, v0_recv, v1_send, v1_recv, v2_send, v2_recv, v3_buf,
    e_part, e1_buf, e2_buf, e3_send, ei_recv, eo_buf,
    m1a, m1b, turned, win, back, ua, ub,
    local_sem, m1a_s, m1a_r, m1b_s, m1b_r, g_s, g_r, v0_s, v0_r, v1_s, v1_r, v2_s, v2_r,
    v3_s, v3_r, e1_s, e1_r, e2_s, e2_r, ei_s, ei_r, eo_s, eo_r, m2_s, m2_r, m3a_s, m3a_r, m3b_s, m3b_r,
):
    d = lax.axis_index("dp")
    t = lax.axis_index("tensor")
    r = lax.axis_index("replica")
    z, q = d // 4, d % 4
    yh, c = q // 2, q % 2
    home_t = z // 2
    half = z % 2

    def at(zz, yy, cc, tt, rr):
        return (zz * 4 + yy * 2 + cc, tt, rr)

    def remote(src, dst, s, rcv, dev):
        return pltpu.make_async_remote_copy(
            src_ref=src, dst_ref=dst, send_sem=s, recv_sem=rcv, device_id=dev, device_id_type=MESH
        )

    def first_block(rr):
        return (5 * rr + 1) // 2

    loads = [
        pltpu.make_async_copy(acts_hbm, acts, local_sem.at[0]),
        pltpu.make_async_copy(grads_hbm, outg, local_sem.at[1]),
        pltpu.make_async_copy(qa_hbm, bases.at[pl.ds(0, HEADS)], local_sem.at[2]),
        pltpu.make_async_copy(qg_hbm, bases.at[pl.ds(HEADS, HEADS)], local_sem.at[3]),
        pltpu.make_async_copy(fac_hbm, fac, local_sem.at[4]),
        pltpu.make_async_copy(parts_hbm, part, local_sem.at[5]),
    ]
    for cp in loads:
        cp.start()

    peers = []
    for k in range(1, R):
        for j in range(2):
            peers.append(at(z, yh, (c + j) % 2, t, (r + k) % R))
    peers.append(at(z, yh, 1 - c, t, r))
    for k in range(1, Z):
        peers.append(at((z + k) % Z, yh, c, t, r))
    for k in range(4):
        for j in range(2):
            if k or j:
                peers.append(at(z, (yh + j) % 2, c, (t + k) % 4, r))
    peers.append(at(z, 1 - yh, 1 - c, t, r))
    barrier = pltpu.get_barrier_semaphore()
    for dev in peers:
        pl.semaphore_signal(barrier, inc=1, device_id=dev, device_id_type=MESH)

    def lookup(s, carry):
        f, u = jnp.int32(0), jnp.int32(0)
        for k in range(FACTORS):
            hit = owner[t, k] == s
            f, u = jnp.where(hit, k, f), jnp.where(hit, 1, u)
        slot_f[s] = f
        slot_u[s] = u
        return carry

    lax.fori_loop(0, SLOTS, lookup, 0)

    for side in range(2):
        src = acts if side == 0 else outg
        loads[side].wait()
        for b in range(HEADS):
            a = src[:, b * BLK:(b + 1) * BLK]
            cov[side * HEADS + b] = contract(a, a, 0, 0)

    def pick(s):
        return cov[slot_f[s]] * slot_u[s].astype(F32)

    def for_sibling(j, carry):
        v0_send[j] = pick(2 * j + 1 - c).astype(BF16)
        return carry

    lax.fori_loop(0, SLOTS // 2, for_sibling, 0)

    pl.semaphore_wait(barrier, len(peers))

    m1 = []
    for k in range(1, R):
        rr = (r + k) % R
        first = pl.multiple_of(first_block(rr) * BLK, BLK)
        m1.append(remote(parts_hbm.at[:, pl.ds(first, 2 * BLK)], m1a.at[r], m1a_s.at[k], m1a_r.at[r], at(z, yh, c, t, rr)))
        m1[-1].start()

        @pl.when(rr % 2 == 0)
        def _():
            third = pl.multiple_of((first_block(rr) + 2) * BLK, BLK)
            remote(parts_hbm.at[:, pl.ds(third, BLK)], m1b.at[r], m1b_s.at[k], m1b_r.at[r], at(z, yh, c, t, rr)).start()

    v0 = remote(v0_send, v0_recv, v0_s, v0_r, at(z, yh, 1 - c, t, r))
    v0.start()

    @pl.when(t == home_t)
    def _():
        for k in range(1, 4):
            remote(qg_hbm.at[pl.ds(5 * half + q, 2)], gwin, g_s.at[k], g_r, at(z, yh, c, (t + k) % 4, r)).start()
        pltpu.make_async_copy(qg_hbm.at[pl.ds(5 * half + q, 2)], gwin, local_sem.at[6]).start()

    loads[2].wait()
    loads[3].wait()
    loads[4].wait()
    e_part[...] = jnp.zeros_like(e_part)
    for f in range(FACTORS):
        src = acts if f < HEADS else outg
        b = f % HEADS
        rot = contract(src[:, b * BLK:(b + 1) * BLK], bases[f], 1, 0)
        at_row = f if f < HEADS else (f + 6 if f < 15 else f + 9)
        e_part[at_row:at_row + 1, :] = jnp.sum(rot * rot, axis=0, keepdims=True) * (DECAY / TOKENS)
    own_f = slot_f[d]
    own_u = slot_u[d].astype(F32)
    own_q = bases[own_f]
    old = fac[...]
    hi = old.astype(BF16)
    rest = old - hi.astype(F32)
    mid = rest.astype(BF16)
    low = (rest - mid.astype(F32)).astype(BF16)
    fq = contract(hi, own_q, 1, 0) + contract(mid, own_q, 1, 0) + contract(low, own_q, 1, 0)
    diag = jnp.sum(own_q.astype(F32) * fq, axis=0, keepdims=True)
    place = own_f + jnp.where(own_f >= 10, 6, 0) + jnp.where(own_f >= 15, 3, 0)
    share = DECAY * own_u * (r == 0).astype(F32)
    rows = lax.broadcasted_iota(jnp.int32, (SLOTS, BLK), 0)
    e_part[...] += jnp.where(rows == place, diag * share, 0.0)

    e1 = []
    own8 = 2 * r + c
    for k in range(1, 8):
        to = (own8 + k) % 8
        e1.append(remote(e_part, e1_buf.at[own8], e1_s.at[k], e1_r.at[own8], at(z, yh, to % 2, t, to // 2)))
        e1[-1].start()

    v0.wait()

    def for_z(j, carry):
        v1_send[j] = (pick(2 * j + c) + v0_recv[j].astype(F32)).astype(BF16)
        return carry

    lax.fori_loop(0, SLOTS // 2, for_z, 0)
    v1 = []
    for k in range(1, Z):
        zz = (z + k) % Z
        v1.append(remote(v1_send.at[pl.ds(2 * zz, 2)], v1_recv.at[z], v1_s.at[k], v1_r.at[z], at(zz, yh, c, t, r)))
        v1[-1].start()

    total = e_part[...]
    for k in range(1, 8):
        frm = (own8 + k) % 8
        remote(e_part, e1_buf.at[frm], e1_s.at[0], e1_r.at[frm], at(z, yh, c, t, r)).wait_recv()
        total += e1_buf[frm]
    e2_buf[z] = total
    e2 = []
    for k in range(1, Z):
        e2.append(remote(e2_buf.at[z], e2_buf.at[z], e2_s.at[k], e2_r.at[z], at((z + k) % Z, yh, c, t, r)))
        e2[-1].start()

    loads[5].wait()
    for k in range(1, R):
        rr = (r + k) % R
        remote(m1a.at[rr], m1a.at[rr], m1a_s.at[0], m1a_r.at[rr], at(z, yh, c, t, r)).wait_recv()

        @pl.when(r % 2 == 0)
        def _():
            remote(m1b.at[rr], m1b.at[rr], m1b_s.at[0], m1b_r.at[rr], at(z, yh, c, t, r)).wait_recv()

    first = first_block(r)
    ids = [first, first + 1, jnp.minimum(first + 2, HEADS - 1)]
    for j in range(3):
        grad = part[:, pl.ds(pl.multiple_of(ids[j] * BLK, BLK), BLK)].astype(F32)
        for k in range(1, R):
            rr = (r + k) % R
            if j < 2:
                grad += m1a[rr, :, j * BLK:(j + 1) * BLK].astype(F32)
            else:
                grad += m1b[rr].astype(F32)
        turned[:, j * BLK:(j + 1) * BLK] = contract(grad.astype(BF16), bases[ids[j]], 1, 0).astype(BF16)

    halo = {
        0: [(128, 32, 0, 1)],
        1: [(0, 96, 160, 0), (96, 64, 0, 2)],
        2: [(64, 96, 0, 3), (0, 64, 192, 1)],
        3: [(0, 32, 224, 2)],
    }

    def halo_copies(me):
        out = []
        for i, (row, n, to_row, to) in enumerate(halo[me]):
            out.append(remote(
                turned.at[pl.ds(row, n)], win.at[pl.ds(to_row, n)],
                m2_s.at[i], m2_r.at[i], at(z, to // 2, to % 2, t, r),
            ))
        return out

    for me in range(4):
        @pl.when(q == me)
        def _():
            for cp in halo_copies(me):
                cp.start()

    win[pl.ds(pl.multiple_of(32 * q, 32), ROWS), :] = turned[...]

    total = e2_buf[z]
    for k in range(1, Z):
        zz = (z + k) % Z
        remote(e2_buf.at[zz], e2_buf.at[zz], e2_s.at[0], e2_r.at[zz], at(z, yh, c, t, r)).wait_recv()
        total += e2_buf[zz]
    e3_send[...] = total
    partner = at(z, 1 - yh, c, t, r)
    ei = remote(e3_send.at[pl.ds(0, 16)], ei_recv, ei_s, ei_r, partner)
    ei.start()
    out_rows = pl.ds(pl.multiple_of(16 + 8 * half, 8), 8)

    @pl.when(t == home_t)
    def _():
        n = 0
        for k in range(4):
            for j in range(2):
                if k or j:
                    remote(
                        e3_send.at[out_rows], eo_buf.at[yh], eo_s.at[n], eo_r.at[yh],
                        at(z, (yh + j) % 2, c, (t + k) % 4, r),
                    ).start()
                    n += 1
        eo_buf[yh] = e3_send[out_rows, :]

    def halo_arrivals(me):
        for src in range(4):
            for i, (row, n, to_row, to) in enumerate(halo[src]):
                if to == me:
                    remote(
                        win.at[pl.ds(to_row, n)], win.at[pl.ds(to_row, n)],
                        m2_s.at[0], m2_r.at[i], at(z, yh, c, t, r),
                    ).wait_recv()

    for me in range(4):
        @pl.when(q == me)
        def _():
            halo_arrivals(me)

    @pl.when(t == home_t)
    def _():
        pltpu.make_async_copy(qg_hbm.at[pl.ds(5 * half + q, 2)], gwin, local_sem.at[6]).wait()

    @pl.when(t != home_t)
    def _():
        remote(gwin, gwin, g_s.at[0], g_r, at(z, yh, c, t, r)).wait_recv()
        remote(eo_buf.at[yh], eo_buf.at[yh], eo_s.at[7], eo_r.at[yh], at(z, yh, c, t, r)).wait_recv()

    ei.wait_recv()
    remote(eo_buf.at[1 - yh], eo_buf.at[1 - yh], eo_s.at[7], eo_r.at[1 - yh], at(z, yh, c, t, r)).wait_recv()

    for b in range(2):
        row = pl.ds(q + b, 1)
        eig_out = eo_buf[0, row, :] + eo_buf[1, row, :]
        eig_col = jnp.transpose(jnp.broadcast_to(eig_out, (BLK, BLK)))
        inner = contract(gwin[b], win[b * BLK:(b + 1) * BLK, :], 0, 0)
        pieces = []
        for j in range(3):
            row_j = pl.ds(ids[j], 1)
            eig_in = e3_send[row_j, :] + ei_recv[row_j, :]
            pieces.append((inner[:, j * BLK:(j + 1) * BLK] / (eig_col * eig_in + DAMPING)).astype(BF16))
        scaled = jnp.concatenate(pieces, axis=1)
        back[b * BLK:(b + 1) * BLK, :] = contract(gwin[b], scaled, 1, 0).astype(BF16)

    own_rows = back[pl.ds(pl.multiple_of(32 * q, 32), ROWS), :]
    for j in range(3):
        upd = contract(own_rows[:, j * BLK:(j + 1) * BLK], bases[ids[j]], 1, 1).astype(BF16)
        if j < 2:
            ua[:, j * BLK:(j + 1) * BLK] = upd
        else:
            ub[...] = upd

    cols_a = pl.ds(pl.multiple_of(first * BLK, BLK), 2 * BLK)
    cols_b = pl.ds(pl.multiple_of(ids[2] * BLK, BLK), BLK)

    def m3a(k):
        return remote(ua, update_hbm.at[:, cols_a], m3a_s.at[k], m3a_r.at[r], at(z, yh, c, t, (r + k) % R))

    def m3b(k):
        return remote(ub, update_hbm.at[:, cols_b], m3b_s.at[k], m3b_r.at[r], at(z, yh, c, t, (r + k) % R))

    for k in range(1, R):
        m3a(k).start()
    pltpu.make_async_copy(ua, update_hbm.at[:, cols_a], local_sem.at[7]).start()

    @pl.when(r % 2 == 0)
    def _():
        for k in range(1, R):
            m3b(k).start()
        pltpu.make_async_copy(ub, update_hbm.at[:, cols_b], local_sem.at[8]).start()

    for k in range(1, Z):
        zz = (z + k) % Z
        remote(v1_recv.at[zz], v1_recv.at[zz], v1_s.at[0], v1_r.at[zz], at(z, yh, c, t, r)).wait_recv()

    def over_z(y):
        acc = v1_send[2 * z + y].astype(F32)
        for k in range(1, Z):
            acc += v1_recv[(z + k) % Z, y].astype(F32)
        return acc

    v2_send[...] = over_z(1 - yh).astype(BF16)
    v2 = remote(v2_send, v2_recv, v2_s, v2_r, partner)
    v2.start()
    kept = over_z(yh)
    v2.wait_recv()
    v3_buf[r] = (kept + v2_recv[...].astype(F32)).astype(BF16)
    v3 = []
    for k in range(1, R):
        v3.append(remote(v3_buf.at[r], v3_buf.at[r], v3_s.at[k], v3_r.at[r], at(z, yh, c, t, (r + k) % R)))
        v3[-1].start()
    for k in range(1, R):
        rr = (r + k) % R
        remote(v3_buf.at[rr], v3_buf.at[rr], v3_s.at[0], v3_r.at[rr], at(z, yh, c, t, r)).wait_recv()
    summed = v3_buf[0].astype(F32)
    for i in range(1, R):
        summed += v3_buf[i].astype(F32)
    refreshed = DECAY * old + (1.0 - DECAY) * (summed * (1.0 / TOKENS))
    fac_out[...] = jnp.where(own_u > 0.0, refreshed, old)

    pltpu.make_async_copy(ua, update_hbm.at[:, cols_a], local_sem.at[7]).wait()
    for k in range(1, R):
        rr = (r + k) % R
        cols = pl.ds(pl.multiple_of(first_block(rr) * BLK, BLK), 2 * BLK)
        remote(ua, update_hbm.at[:, cols], m3a_s.at[0], m3a_r.at[rr], at(z, yh, c, t, r)).wait_recv()

        @pl.when(rr % 2 == 0)
        def _():
            cols3 = pl.ds(pl.multiple_of((first_block(rr) + 2) * BLK, BLK), BLK)
            remote(ub, update_hbm.at[:, cols3], m3b_s.at[0], m3b_r.at[rr], at(z, yh, c, t, r)).wait_recv()

    for k in range(1, R):
        m1[k - 1].wait_send()
        m3a(k).wait_send()
        v3[k - 1].wait_send()
        rr = (r + k) % R

        @pl.when(rr % 2 == 0)
        def _():
            remote(m1b.at[0], m1b.at[0], m1b_s.at[k], m1b_r.at[0], at(z, yh, c, t, r)).wait_send()

        @pl.when(r % 2 == 0)
        def _():
            m3b(k).wait_send()

    @pl.when(r % 2 == 0)
    def _():
        pltpu.make_async_copy(ub, update_hbm.at[:, cols_b], local_sem.at[8]).wait()

    @pl.when(t == home_t)
    def _():
        for k in range(1, 4):
            remote(gwin, gwin, g_s.at[k], g_r, at(z, yh, c, t, r)).wait_send()
        for n in range(7):
            remote(e3_send.at[out_rows], eo_buf.at[yh], eo_s.at[n], eo_r.at[yh], at(z, yh, c, t, r)).wait_send()

    for cp in e1 + e2 + v1 + [ei, v2]:
        cp.wait_send()
    for me in range(4):
        @pl.when(q == me)
        def _():
            for cp in halo_copies(me):
                cp.wait_send()


def per_device(acts, out_grads, grad_parts, basis_a, basis_g, fac_old, owner_slot):
    sem = pltpu.SemaphoreType.DMA
    half_slots = SLOTS // 2
    hbm = pl.BlockSpec(memory_space=pl.ANY)
    update, fac_new = pl.pallas_call(
        kernel,
        out_shape=(
            jax.ShapeDtypeStruct((ROWS, HEADS * BLK), BF16),
            jax.ShapeDtypeStruct((BLK, BLK), F32),
        ),
        in_specs=[pl.BlockSpec(memory_space=pltpu.SMEM)] + [hbm] * 6,
        out_specs=(hbm, pl.BlockSpec(memory_space=pltpu.VMEM)),
        scratch_shapes=[
            pltpu.VMEM((256, HEADS * BLK), BF16),
            pltpu.VMEM((256, HEADS * BLK), BF16),
            pltpu.VMEM((ROWS, HEADS * BLK), BF16),
            pltpu.VMEM((FACTORS, BLK, BLK), BF16),
            pltpu.VMEM((BLK, BLK), F32),
            pltpu.VMEM((2, BLK, BLK), BF16),
            pltpu.VMEM((FACTORS, BLK, BLK), F32),
            pltpu.SMEM((SLOTS,), jnp.int32),
            pltpu.SMEM((SLOTS,), jnp.int32),
            pltpu.VMEM((half_slots, BLK, BLK), BF16),
            pltpu.VMEM((half_slots, BLK, BLK), BF16),
            pltpu.VMEM((half_slots, BLK, BLK), BF16),
            pltpu.VMEM((Z, 2, BLK, BLK), BF16),
            pltpu.VMEM((BLK, BLK), BF16),
            pltpu.VMEM((BLK, BLK), BF16),
            pltpu.VMEM((R, BLK, BLK), BF16),
            pltpu.VMEM((SLOTS, BLK), F32),
            pltpu.VMEM((8, SLOTS, BLK), F32),
            pltpu.VMEM((Z, SLOTS, BLK), F32),
            pltpu.VMEM((SLOTS, BLK), F32),
            pltpu.VMEM((16, BLK), F32),
            pltpu.VMEM((2, 8, BLK), F32),
            pltpu.VMEM((R, ROWS, 2 * BLK), BF16),
            pltpu.VMEM((R, ROWS, BLK), BF16),
            pltpu.VMEM((ROWS, 3 * BLK), BF16),
            pltpu.VMEM((WIN, 3 * BLK), BF16),
            pltpu.VMEM((WIN, 3 * BLK), BF16),
            pltpu.VMEM((ROWS, 2 * BLK), BF16),
            pltpu.VMEM((ROWS, BLK), BF16),
            sem((9,)),
            sem((R,)), sem((R,)), sem((R,)), sem((R,)),
            sem((4,)), sem,
            sem, sem,
            sem((Z,)), sem((Z,)),
            sem, sem,
            sem((R,)), sem((R,)),
            sem((8,)), sem((8,)),
            sem((Z,)), sem((Z,)),
            sem, sem,
            sem((8,)), sem((2,)),
            sem((2,)), sem((2,)),
            sem((R,)), sem((R,)), sem((R,)), sem((R,)),
        ],
        compiler_params=pltpu.CompilerParams(
            collective_id=0, has_side_effects=True, vmem_limit_bytes=32 * 1024 * 1024
        ),
    )(owner_slot, acts, out_grads, grad_parts[0], basis_a, basis_g, fac_old[0, 0])
    return update, fac_new[None, None]


def solution(mesh):
    placed = (
        P(("dp", "replica"), "tensor"),
        P(("dp", "replica"), "tensor"),
        P("replica", "dp", "tensor"),
        P("tensor", None, None),
        P("tensor", None, None),
        P("tensor", "dp", None, None),
        P(),
    )
    return jax.shard_map(
        per_device,
        mesh=mesh,
        in_specs=placed,
        out_specs=(P("dp", "tensor"), P("tensor", "dp", None, None)),
        check_vma=False,
    )
```

```python
import jax
import jax.numpy as jnp
from jax import lax
from jax.experimental import pallas as pl
from jax.experimental.pallas import tpu as pltpu
from jax.sharding import PartitionSpec as P

MESH = pl.DeviceIdType.MESH
F32, BF16 = jnp.float32, jnp.bfloat16

DECAY = 0.5
DAMPING = 0.01
TOKENS = 32768
BLK = 128
HEADS = 10
FACTORS = 2 * HEADS
ROWS = 160
WIN = 2 * BLK
SLOTS = 32
Z, R = 8, 4
QR = BLK // R


def contract(a, b, da, db):
    return lax.dot_general(a, b, (((da,), (db,)), ((), ())), preferred_element_type=F32)


def kernel(
    owner, acts_hbm, grads_hbm, parts_hbm, qa_hbm, qg_hbm, fac_hbm,
    update_hbm, fac_out,
    acts, outg, part, bases, fac, gwin, cov, slot_f, slot_u,
    v0_send, v0_recv, v1_buf, v1_recv, v2_send, v2_recv, v3_buf,
    e_part, e1_buf, e2_buf, e3_send, ei_buf, eo_buf,
    m1a, m1b, turned, win, back, ua, ub,
    local_sem, m1a_s, m1a_r, m1b_s, m1b_r, g_s, g_r, v0_s, v0_r, v1_s, v1_r, v2_s, v2_r,
    v3_s, v3_r, e1_s, e1_r, e2_s, e2_r, ei_s, ei_r, eo_s, eo_r, m2_s, m2_r, m3a_s, m3a_r, m3b_s, m3b_r,
):
    d = lax.axis_index("dp")
    t = lax.axis_index("tensor")
    r = lax.axis_index("replica")
    z, q = d // 4, d % 4
    yh, c = q // 2, q % 2
    home_t = z // 2
    half = z % 2

    def at(zz, yy, cc, tt, rr):
        return (zz * 4 + yy * 2 + cc, tt, rr)

    me_dev = at(z, yh, c, t, r)

    def remote(src, dst, s, rcv, dev):
        return pltpu.make_async_remote_copy(
            src_ref=src, dst_ref=dst, send_sem=s, recv_sem=rcv, device_id=dev, device_id_type=MESH
        )

    def arrived(dst, rcv, s):
        remote(dst, dst, s, rcv, me_dev).wait_recv()

    def first_block(rr):
        return (5 * rr + 1) // 2

    loads = [
        pltpu.make_async_copy(acts_hbm, acts, local_sem.at[0]),
        pltpu.make_async_copy(grads_hbm, outg, local_sem.at[1]),
        pltpu.make_async_copy(qa_hbm, bases.at[pl.ds(0, HEADS)], local_sem.at[2]),
        pltpu.make_async_copy(qg_hbm, bases.at[pl.ds(HEADS, HEADS)], local_sem.at[3]),
        pltpu.make_async_copy(fac_hbm, fac, local_sem.at[4]),
        pltpu.make_async_copy(parts_hbm, part, local_sem.at[5]),
    ]
    for cp in loads:
        cp.start()

    peers = []
    for k in range(1, R):
        for j in range(2):
            peers.append(at(z, yh, (c + j) % 2, t, (r + k) % R))
    for k in range(4):
        for j in range(2):
            for i in range(2):
                if k or j or i:
                    peers.append(at(z, (yh + j) % 2, (c + i) % 2, (t + k) % 4, r))
    for k in range(1, Z):
        for j in range(2):
            peers.append(at((z + k) % Z, (yh + j) % 2, c, t, r))
    barrier = pltpu.get_barrier_semaphore()
    for dev in peers:
        pl.semaphore_signal(barrier, inc=1, device_id=dev, device_id_type=MESH)

    def lookup(s, carry):
        f, u = jnp.int32(0), jnp.int32(0)
        for k in range(FACTORS):
            hit = owner[t, k] == s
            f, u = jnp.where(hit, k, f), jnp.where(hit, 1, u)
        slot_f[s] = f
        slot_u[s] = u
        return carry

    lax.fori_loop(0, SLOTS, lookup, 0)

    for side in range(2):
        src = acts if side == 0 else outg
        loads[side].wait()
        for b in range(HEADS):
            a = src[:, b * BLK:(b + 1) * BLK]
            cov[side * HEADS + b] = contract(a, a, 0, 0)

    def pick(s):
        return cov[slot_f[s]] * slot_u[s].astype(F32)

    def for_sibling(j, carry):
        v0_send[j] = pick(2 * j + 1 - c).astype(BF16)
        return carry

    lax.fori_loop(0, SLOTS // 2, for_sibling, 0)

    loads[2].wait()
    loads[3].wait()
    loads[4].wait()
    e_part[...] = jnp.zeros_like(e_part)
    for f in range(FACTORS):
        src = acts if f < HEADS else outg
        b = f % HEADS
        rot = contract(src[:, b * BLK:(b + 1) * BLK], bases[f], 1, 0)
        at_row = f if f < HEADS else (f + 6 if f < 15 else f + 9)
        e_part[at_row:at_row + 1, :] = jnp.sum(rot * rot, axis=0, keepdims=True) * (DECAY / TOKENS)
    own_f = slot_f[d]
    own_u = slot_u[d].astype(F32)
    own_q = bases[own_f]
    old = fac[...]
    hi = old.astype(BF16)
    rest = old - hi.astype(F32)
    mid = rest.astype(BF16)
    low = (rest - mid.astype(F32)).astype(BF16)
    fq = contract(hi, own_q, 1, 0) + contract(mid, own_q, 1, 0) + contract(low, own_q, 1, 0)
    diag = jnp.sum(own_q.astype(F32) * fq, axis=0, keepdims=True)
    place = own_f + jnp.where(own_f >= 10, 6, 0) + jnp.where(own_f >= 15, 3, 0)
    share = DECAY * own_u * (r == 0).astype(F32)
    rows = lax.broadcasted_iota(jnp.int32, (SLOTS, BLK), 0)
    e_part[...] += jnp.where(rows == place, diag * share, 0.0)

    pl.semaphore_wait(barrier, len(peers))

    v0 = remote(v0_send, v0_recv, v0_s, v0_r, at(z, yh, 1 - c, t, r))
    v0.start()

    e1 = []
    own8 = 2 * r + c
    for k in range(1, 8):
        to = (own8 + k) % 8
        rows_to = pl.ds(pl.multiple_of(16 * (to % 2), 16), 16)
        e1.append(remote(e_part.at[rows_to], e1_buf.at[own8], e1_s.at[k], e1_r.at[own8], at(z, yh, to % 2, t, to // 2)))
        e1[-1].start()

    m1 = []
    for k in range(1, R):
        rr = (r + k) % R
        first = pl.multiple_of(first_block(rr) * BLK, BLK)
        m1.append(remote(parts_hbm.at[:, pl.ds(first, 2 * BLK)], m1a.at[r], m1a_s.at[k], m1a_r.at[r], at(z, yh, c, t, rr)))
        m1[-1].start()

        @pl.when(rr % 2 == 0)
        def _():
            third = pl.multiple_of((first_block(rr) + 2) * BLK, BLK)
            remote(parts_hbm.at[:, pl.ds(third, BLK)], m1b.at[r], m1b_s.at[k], m1b_r.at[r], at(z, yh, c, t, rr)).start()

    @pl.when(t == home_t)
    def _():
        for k in range(1, 4):
            remote(qg_hbm.at[pl.ds(5 * half + q, 2)], gwin, g_s.at[k], g_r, at(z, yh, c, (t + k) % 4, r)).start()
        pltpu.make_async_copy(qg_hbm.at[pl.ds(5 * half + q, 2)], gwin, local_sem.at[6]).start()

    v0.wait()

    def for_x(j, carry):
        both = (pick(2 * j + c) + v0_recv[j].astype(F32)).astype(BF16)
        for i in range(R):
            v1_buf[i, j] = both[i * QR:(i + 1) * QR]
        return carry

    lax.fori_loop(0, SLOTS // 2, for_x, 0)
    v1 = []
    for k in range(1, R):
        rr = (r + k) % R
        v1.append(remote(v1_buf.at[rr], v1_recv.at[r], v1_s.at[k], v1_r.at[r], at(z, yh, c, t, rr)))
        v1[-1].start()

    total = e_part[pl.ds(pl.multiple_of(16 * c, 16), 16), :]
    for k in range(1, 8):
        frm = (own8 + k) % 8
        arrived(e1_buf.at[frm], e1_r.at[frm], e1_s.at[0])
        total += e1_buf[frm]
    e2_buf[z] = total
    e2 = []
    for k in range(1, Z):
        e2.append(remote(e2_buf.at[z], e2_buf.at[z], e2_s.at[k], e2_r.at[z], at((z + k) % Z, yh, c, t, r)))
        e2[-1].start()

    loads[5].wait()
    for k in range(1, R):
        rr = (r + k) % R
        arrived(m1a.at[rr], m1a_r.at[rr], m1a_s.at[0])

        @pl.when(r % 2 == 0)
        def _():
            arrived(m1b.at[rr], m1b_r.at[rr], m1b_s.at[0])

    first = first_block(r)
    ids = [first, first + 1, jnp.minimum(first + 2, HEADS - 1)]
    for j in range(3):
        grad = part[:, pl.ds(pl.multiple_of(ids[j] * BLK, BLK), BLK)].astype(F32)
        for k in range(1, R):
            rr = (r + k) % R
            if j < 2:
                grad += m1a[rr, :, j * BLK:(j + 1) * BLK].astype(F32)
            else:
                grad += m1b[rr].astype(F32)
        turned[:, j * BLK:(j + 1) * BLK] = contract(grad.astype(BF16), bases[ids[j]], 1, 0).astype(BF16)

    halo = {
        0: [(128, 32, 0, 1)],
        1: [(0, 96, 160, 0), (96, 64, 0, 2)],
        2: [(64, 96, 0, 3), (0, 64, 192, 1)],
        3: [(0, 32, 224, 2)],
    }

    def halo_copies(me):
        out = []
        for i, (row, n, to_row, to) in enumerate(halo[me]):
            out.append(remote(
                turned.at[pl.ds(row, n)], win.at[pl.ds(to_row, n)],
                m2_s.at[i], m2_r.at[i], at(z, to // 2, to % 2, t, r),
            ))
        return out

    for me in range(4):
        @pl.when(q == me)
        def _():
            for cp in halo_copies(me):
                cp.start()

    win[pl.ds(pl.multiple_of(32 * q, 32), ROWS), :] = turned[...]

    for k in range(1, R):
        rr = (r + k) % R
        arrived(v1_recv.at[rr], v1_r.at[rr], v1_s.at[0])

    def over_x(j, carry):
        acc = v1_buf[r, j].astype(F32)
        for k in range(1, R):
            acc += v1_recv[(r + k) % R, j].astype(F32)
        v2_send[j] = acc.astype(BF16)
        return carry

    lax.fori_loop(0, SLOTS // 2, over_x, 0)
    v2 = []
    own16 = 2 * z + yh
    for k in range(1, 16):
        to = (own16 + k) % 16
        v2.append(remote(v2_send.at[to], v2_recv.at[own16], v2_s.at[k], v2_r.at[own16], at(to // 2, to % 2, c, t, r)))
        v2[-1].start()

    total = e2_buf[z]
    for k in range(1, Z):
        zz = (z + k) % Z
        arrived(e2_buf.at[zz], e2_r.at[zz], e2_s.at[0])
        total += e2_buf[zz]
    e3_send[...] = total
    out_rows = pl.ds(pl.multiple_of(8 * half, 8), 8)

    def share_in(k):
        y_to, c_to = (yh + k // 2) % 2, k % 2
        return remote(e3_send, ei_buf.at[yh], ei_s.at[k], ei_r.at[yh], at(z, y_to, c_to, t, r))

    def share_out(k):
        y_to, c_to, t_to = (yh + (k // 2) % 2) % 2, (1 + k) % 2, (t + k // 4) % 4
        return remote(e3_send.at[out_rows], eo_buf.at[yh], eo_s.at[k], eo_r.at[yh], at(z, y_to, c_to, t_to, r))

    @pl.when(c == 0)
    def _():
        for k in range(1, 4):
            share_in(k).start()
        ei_buf[yh] = e3_send[...]

    @pl.when((c == 1) & (t == home_t))
    def _():
        for k in range(1, 16):
            share_out(k).start()
        eo_buf[yh] = e3_send[out_rows, :]

    def halo_arrivals(me):
        for src in range(4):
            for i, (row, n, to_row, to) in enumerate(halo[src]):
                if to == me:
                    arrived(win.at[pl.ds(to_row, n)], m2_r.at[i], m2_s.at[0])

    for me in range(4):
        @pl.when(q == me)
        def _():
            halo_arrivals(me)

    @pl.when(t == home_t)
    def _():
        pltpu.make_async_copy(qg_hbm.at[pl.ds(5 * half + q, 2)], gwin, local_sem.at[6]).wait()

    @pl.when(t != home_t)
    def _():
        arrived(gwin, g_r, g_s.at[0])

    @pl.when(c == 1)
    def _():
        arrived(ei_buf.at[yh], ei_r.at[yh], ei_s.at[0])

    @pl.when((c == 0) | (t != home_t))
    def _():
        arrived(eo_buf.at[yh], eo_r.at[yh], eo_s.at[0])

    arrived(ei_buf.at[1 - yh], ei_r.at[1 - yh], ei_s.at[0])
    arrived(eo_buf.at[1 - yh], eo_r.at[1 - yh], eo_s.at[0])

    for b in range(2):
        row = pl.ds(q + b, 1)
        eig_out = eo_buf[0, row, :] + eo_buf[1, row, :]
        eig_col = jnp.transpose(jnp.broadcast_to(eig_out, (BLK, BLK)))
        inner = contract(gwin[b], win[b * BLK:(b + 1) * BLK, :], 0, 0)
        pieces = []
        for j in range(3):
            row_j = pl.ds(ids[j], 1)
            eig_in = ei_buf[0, row_j, :] + ei_buf[1, row_j, :]
            pieces.append((inner[:, j * BLK:(j + 1) * BLK] / (eig_col * eig_in + DAMPING)).astype(BF16))
        scaled = jnp.concatenate(pieces, axis=1)
        back[b * BLK:(b + 1) * BLK, :] = contract(gwin[b], scaled, 1, 0).astype(BF16)

    own_rows = back[pl.ds(pl.multiple_of(32 * q, 32), ROWS), :]
    for j in range(3):
        upd = contract(own_rows[:, j * BLK:(j + 1) * BLK], bases[ids[j]], 1, 1).astype(BF16)
        if j < 2:
            ua[:, j * BLK:(j + 1) * BLK] = upd
        else:
            ub[...] = upd

    cols_a = pl.ds(pl.multiple_of(first * BLK, BLK), 2 * BLK)
    cols_b = pl.ds(pl.multiple_of(ids[2] * BLK, BLK), BLK)

    def m3a(k):
        return remote(ua, update_hbm.at[:, cols_a], m3a_s.at[k], m3a_r.at[r], at(z, yh, c, t, (r + k) % R))

    def m3b(k):
        return remote(ub, update_hbm.at[:, cols_b], m3b_s.at[k], m3b_r.at[r], at(z, yh, c, t, (r + k) % R))

    for k in range(1, R):
        m3a(k).start()
    pltpu.make_async_copy(ua, update_hbm.at[:, cols_a], local_sem.at[7]).start()

    @pl.when(r % 2 == 0)
    def _():
        for k in range(1, R):
            m3b(k).start()
        pltpu.make_async_copy(ub, update_hbm.at[:, cols_b], local_sem.at[8]).start()

    acc = v2_send[own16].astype(F32)
    for k in range(1, 16):
        frm = (own16 + k) % 16
        arrived(v2_recv.at[frm], v2_r.at[frm], v2_s.at[0])
        acc += v2_recv[frm].astype(F32)
    v3_buf[r] = acc.astype(BF16)
    v3 = []
    for k in range(1, R):
        v3.append(remote(v3_buf.at[r], v3_buf.at[r], v3_s.at[k], v3_r.at[r], at(z, yh, c, t, (r + k) % R)))
        v3[-1].start()
    for k in range(1, R):
        rr = (r + k) % R
        arrived(v3_buf.at[rr], v3_r.at[rr], v3_s.at[0])
    for i in range(R):
        old_rows = fac[i * QR:(i + 1) * QR, :]
        refreshed = DECAY * old_rows + (1.0 - DECAY) * (v3_buf[i].astype(F32) * (1.0 / TOKENS))
        fac_out[i * QR:(i + 1) * QR, :] = jnp.where(own_u > 0.0, refreshed, old_rows)

    pltpu.make_async_copy(ua, update_hbm.at[:, cols_a], local_sem.at[7]).wait()
    for k in range(1, R):
        rr = (r + k) % R
        cols = pl.ds(pl.multiple_of(first_block(rr) * BLK, BLK), 2 * BLK)
        arrived(update_hbm.at[:, cols], m3a_r.at[rr], m3a_s.at[0])

        @pl.when(rr % 2 == 0)
        def _():
            cols3 = pl.ds(pl.multiple_of((first_block(rr) + 2) * BLK, BLK), BLK)
            arrived(update_hbm.at[:, cols3], m3b_r.at[rr], m3b_s.at[0])

    for k in range(1, R):
        m1[k - 1].wait_send()
        m3a(k).wait_send()
        rr = (r + k) % R

        @pl.when(rr % 2 == 0)
        def _():
            remote(m1b.at[0], m1b.at[0], m1b_s.at[k], m1b_r.at[0], me_dev).wait_send()

        @pl.when(r % 2 == 0)
        def _():
            m3b(k).wait_send()

    @pl.when(r % 2 == 0)
    def _():
        pltpu.make_async_copy(ub, update_hbm.at[:, cols_b], local_sem.at[8]).wait()

    @pl.when(t == home_t)
    def _():
        for k in range(1, 4):
            remote(gwin, gwin, g_s.at[k], g_r, me_dev).wait_send()

    @pl.when(c == 0)
    def _():
        for k in range(1, 4):
            share_in(k).wait_send()

    @pl.when((c == 1) & (t == home_t))
    def _():
        for k in range(1, 16):
            share_out(k).wait_send()

    for cp in e1 + e2 + v1 + v2 + v3:
        cp.wait_send()
    for me in range(4):
        @pl.when(q == me)
        def _():
            for cp in halo_copies(me):
                cp.wait_send()


def per_device(acts, out_grads, grad_parts, basis_a, basis_g, fac_old, owner_slot):
    sem = pltpu.SemaphoreType.DMA
    half_slots = SLOTS // 2
    hbm = pl.BlockSpec(memory_space=pl.ANY)
    update, fac_new = pl.pallas_call(
        kernel,
        out_shape=(
            jax.ShapeDtypeStruct((ROWS, HEADS * BLK), BF16),
            jax.ShapeDtypeStruct((BLK, BLK), F32),
        ),
        in_specs=[pl.BlockSpec(memory_space=pltpu.SMEM)] + [hbm] * 6,
        out_specs=(hbm, pl.BlockSpec(memory_space=pltpu.VMEM)),
        scratch_shapes=[
            pltpu.VMEM((256, HEADS * BLK), BF16),
            pltpu.VMEM((256, HEADS * BLK), BF16),
            pltpu.VMEM((ROWS, HEADS * BLK), BF16),
            pltpu.VMEM((FACTORS, BLK, BLK), BF16),
            pltpu.VMEM((BLK, BLK), F32),
            pltpu.VMEM((2, BLK, BLK), BF16),
            pltpu.VMEM((FACTORS, BLK, BLK), F32),
            pltpu.SMEM((SLOTS,), jnp.int32),
            pltpu.SMEM((SLOTS,), jnp.int32),
            pltpu.VMEM((half_slots, BLK, BLK), BF16),
            pltpu.VMEM((half_slots, BLK, BLK), BF16),
            pltpu.VMEM((R, half_slots, QR, BLK), BF16),
            pltpu.VMEM((R, half_slots, QR, BLK), BF16),
            pltpu.VMEM((half_slots, QR, BLK), BF16),
            pltpu.VMEM((half_slots, QR, BLK), BF16),
            pltpu.VMEM((R, QR, BLK), BF16),
            pltpu.VMEM((SLOTS, BLK), F32),
            pltpu.VMEM((8, 16, BLK), F32),
            pltpu.VMEM((Z, 16, BLK), F32),
            pltpu.VMEM((16, BLK), F32),
            pltpu.VMEM((2, 16, BLK), F32),
            pltpu.VMEM((2, 8, BLK), F32),
            pltpu.VMEM((R, ROWS, 2 * BLK), BF16),
            pltpu.VMEM((R, ROWS, BLK), BF16),
            pltpu.VMEM((ROWS, 3 * BLK), BF16),
            pltpu.VMEM((WIN, 3 * BLK), BF16),
            pltpu.VMEM((WIN, 3 * BLK), BF16),
            pltpu.VMEM((ROWS, 2 * BLK), BF16),
            pltpu.VMEM((ROWS, BLK), BF16),
            sem((9,)),
            sem((R,)), sem((R,)), sem((R,)), sem((R,)),
            sem((4,)), sem,
            sem, sem,
            sem((R,)), sem((R,)),
            sem((16,)), sem((16,)),
            sem((R,)), sem((R,)),
            sem((8,)), sem((8,)),
            sem((Z,)), sem((Z,)),
            sem((4,)), sem((2,)),
            sem((16,)), sem((2,)),
            sem((2,)), sem((2,)),
            sem((R,)), sem((R,)), sem((R,)), sem((R,)),
        ],
        compiler_params=pltpu.CompilerParams(
            collective_id=0, has_side_effects=True, vmem_limit_bytes=60 * 1024 * 1024
        ),
    )(owner_slot, acts, out_grads, grad_parts[0], basis_a, basis_g, fac_old[0, 0])
    return update, fac_new[None, None]


def solution(mesh):
    placed = (
        P(("dp", "replica"), "tensor"),
        P(("dp", "replica"), "tensor"),
        P("replica", "dp", "tensor"),
        P("tensor", None, None),
        P("tensor", None, None),
        P("tensor", "dp", None, None),
        P(),
    )
    return jax.shard_map(
        per_device,
        mesh=mesh,
        in_specs=placed,
        out_specs=(P("dp", "tensor"), P("tensor", "dp", None, None)),
        check_vma=False,
    )
```

```python
import jax
import jax.numpy as jnp
from jax import lax
from jax.experimental import pallas as pl
from jax.experimental.pallas import tpu as pltpu
from jax.sharding import PartitionSpec as P

MESH = pl.DeviceIdType.MESH
F32, BF16 = jnp.float32, jnp.bfloat16

DECAY = 0.5
DAMPING = 0.01
TOKENS = 32768
BLK = 128
HEADS = 10
FACTORS = 2 * HEADS
ROWS = 160
WIN = 2 * BLK
SLOTS = 32
Z, R = 8, 4
QR = BLK // R
X_ORDER = (2, 1, 3)
Z_ORDER = (4, 3, 5, 2, 6, 1, 7)
PAIRS = Z_ORDER + (0,)
PART = SLOTS // 4


def contract(a, b, da, db):
    return lax.dot_general(a, b, (((da,), (db,)), ((), ())), preferred_element_type=F32)


def kernel(
    owner, acts_hbm, grads_hbm, parts_hbm, qa_hbm, qg_hbm, fac_hbm,
    update_hbm, fac_out,
    acts, outg, part, bases, fac, gwin, cov, slot_f, slot_u,
    v0_send, v0_recv, v1_buf, v1_recv, v2_send, v2_recv, vy_send, vy_recv, v3_buf,
    e_part, e1_buf, e2_buf, e3_send, ei_buf, eo_buf,
    m1a, m1b, turned, win, back, upd,
    local_sem, m1a_s, m1a_r, m1b_s, m1b_r, g_s, g_r, v0_s, v0_r, v1_s, v1_r, v2_s, v2_r, vy_s, vy_r,
    v3_s, v3_r, e1_s, e1_r, e2_s, e2_r, ei_s, ei_r, eo_s, eo_r, m2_s, m2_r, m3_s, m3_r,
):
    d = lax.axis_index("dp")
    t = lax.axis_index("tensor")
    r = lax.axis_index("replica")
    z, q = d // 4, d % 4
    yh, c = q // 2, q % 2
    home_t = z // 2
    half = z % 2

    def at(zz, yy, cc, tt, rr):
        return (zz * 4 + yy * 2 + cc, tt, rr)

    me_dev = at(z, yh, c, t, r)

    def remote(src, dst, s, rcv, dev):
        return pltpu.make_async_remote_copy(
            src_ref=src, dst_ref=dst, send_sem=s, recv_sem=rcv, device_id=dev, device_id_type=MESH
        )

    def arrived(dst, rcv, s):
        remote(dst, dst, s, rcv, me_dev).wait_recv()

    def first_block(rr):
        return (5 * rr + 1) // 2

    loads = [
        pltpu.make_async_copy(acts_hbm, acts, local_sem.at[0]),
        pltpu.make_async_copy(grads_hbm, outg, local_sem.at[1]),
        pltpu.make_async_copy(qa_hbm, bases.at[pl.ds(0, HEADS)], local_sem.at[2]),
        pltpu.make_async_copy(qg_hbm, bases.at[pl.ds(HEADS, HEADS)], local_sem.at[3]),
        pltpu.make_async_copy(fac_hbm, fac, local_sem.at[4]),
        pltpu.make_async_copy(parts_hbm, part, local_sem.at[5]),
    ]
    for cp in loads:
        cp.start()

    peers = []
    for k in range(1, R):
        for j in range(2):
            peers.append(at(z, yh, (c + j) % 2, t, (r + k) % R))
    for k in range(4):
        for j in range(2):
            for i in range(2):
                if k or j or i:
                    peers.append(at(z, (yh + j) % 2, (c + i) % 2, (t + k) % 4, r))
    for k in range(1, Z):
        peers.append(at((z + k) % Z, yh, c, t, r))
    barrier = pltpu.get_barrier_semaphore()
    for dev in peers:
        pl.semaphore_signal(barrier, inc=1, device_id=dev, device_id_type=MESH)

    def lookup(s, carry):
        f, u = jnp.int32(0), jnp.int32(0)
        for k in range(FACTORS):
            hit = owner[t, k] == s
            f, u = jnp.where(hit, k, f), jnp.where(hit, 1, u)
        slot_f[s] = f
        slot_u[s] = u
        return carry

    lax.fori_loop(0, SLOTS, lookup, 0)

    for side in range(2):
        src = acts if side == 0 else outg
        loads[side].wait()
        for b in range(HEADS):
            a = src[:, b * BLK:(b + 1) * BLK]
            cov[side * HEADS + b] = contract(a, a, 0, 0)

    def pick(s):
        return cov[slot_f[s]] * slot_u[s].astype(F32)

    def slot(j, core):
        return (z + PAIRS[j // 2]) % Z * 4 + j % 2 * 2 + core

    for j in range(SLOTS // 2):
        v0_send[j] = pick(slot(j, 1 - c)).astype(BF16)

    loads[2].wait()
    loads[3].wait()
    loads[4].wait()
    e_part[...] = jnp.zeros_like(e_part)
    for f in range(FACTORS):
        src = acts if f < HEADS else outg
        b = f % HEADS
        rot = contract(src[:, b * BLK:(b + 1) * BLK], bases[f], 1, 0)
        at_row = f if f < HEADS else (f + 6 if f < 15 else f + 9)
        e_part[at_row:at_row + 1, :] = jnp.sum(rot * rot, axis=0, keepdims=True) * (DECAY / TOKENS)
    own_f = slot_f[d]
    own_u = slot_u[d].astype(F32)
    own_q = bases[own_f]
    old = fac[...]
    hi = old.astype(BF16)
    rest = old - hi.astype(F32)
    mid = rest.astype(BF16)
    low = (rest - mid.astype(F32)).astype(BF16)
    fq = contract(hi, own_q, 1, 0) + contract(mid, own_q, 1, 0) + contract(low, own_q, 1, 0)
    diag = jnp.sum(own_q.astype(F32) * fq, axis=0, keepdims=True)
    place = own_f + jnp.where(own_f >= 10, 6, 0) + jnp.where(own_f >= 15, 3, 0)
    share = DECAY * own_u * (r == 0).astype(F32)
    rows = lax.broadcasted_iota(jnp.int32, (SLOTS, BLK), 0)
    e_part[...] += jnp.where(rows == place, diag * share, 0.0)

    pl.semaphore_wait(barrier, len(peers))

    v0 = []
    for h in range(2):
        part_h = pl.ds(h * PART, PART)
        v0.append(remote(v0_send.at[part_h], v0_recv.at[part_h], v0_s.at[h], v0_r.at[h], at(z, yh, 1 - c, t, r)))
        v0[-1].start()

    e1 = []
    own8 = 2 * r + c
    for k in range(1, 8):
        to = (own8 + k) % 8
        rows_to = pl.ds(pl.multiple_of(16 * (to % 2), 16), 16)
        e1.append(remote(e_part.at[rows_to], e1_buf.at[own8], e1_s.at[k], e1_r.at[own8], at(z, yh, to % 2, t, to // 2)))
        e1[-1].start()

    m1 = []
    for k in range(1, R):
        rr = (r + k) % R
        first = pl.multiple_of(first_block(rr) * BLK, BLK)
        m1.append(remote(parts_hbm.at[:, pl.ds(first, 2 * BLK)], m1a.at[r], m1a_s.at[k], m1a_r.at[r], at(z, yh, c, t, rr)))
        m1[-1].start()

        @pl.when(rr % 2 == 0)
        def _():
            third = pl.multiple_of((first_block(rr) + 2) * BLK, BLK)
            remote(parts_hbm.at[:, pl.ds(third, BLK)], m1b.at[r], m1b_s.at[k], m1b_r.at[r], at(z, yh, c, t, rr)).start()

    @pl.when(t == home_t)
    def _():
        for k in range(1, 4):
            remote(qg_hbm.at[pl.ds(5 * half + q, 2)], gwin, g_s.at[k], g_r, at(z, yh, c, (t + k) % 4, r)).start()
        pltpu.make_async_copy(qg_hbm.at[pl.ds(5 * half + q, 2)], gwin, local_sem.at[6]).start()

    v1 = []
    for h in range(2):
        v0[h].wait_recv()
        for j in range(h * PART, (h + 1) * PART):
            both = (pick(slot(j, c)) + v0_recv[j].astype(F32)).astype(BF16)
            for i in range(R):
                v1_buf[i, j] = both[i * QR:(i + 1) * QR]
        part_h = pl.ds(h * PART, PART)
        for k in X_ORDER:
            rr = (r + k) % R
            v1.append(remote(
                v1_buf.at[rr, part_h], v1_recv.at[r, part_h],
                v1_s.at[h, k], v1_r.at[h, r], at(z, yh, c, t, rr),
            ))
            v1[-1].start()

    total = e_part[pl.ds(pl.multiple_of(16 * c, 16), 16), :]
    for k in range(1, 8):
        frm = (own8 + k) % 8
        arrived(e1_buf.at[frm], e1_r.at[frm], e1_s.at[0])
        total += e1_buf[frm]
    e2_buf[z] = total
    e2 = []
    for k in Z_ORDER:
        e2.append(remote(e2_buf.at[z], e2_buf.at[z], e2_s.at[k], e2_r.at[z], at((z + k) % Z, yh, c, t, r)))
        e2[-1].start()

    loads[5].wait()
    for k in range(1, R):
        rr = (r + k) % R
        arrived(m1a.at[rr], m1a_r.at[rr], m1a_s.at[0])

        @pl.when(r % 2 == 0)
        def _():
            arrived(m1b.at[rr], m1b_r.at[rr], m1b_s.at[0])

    first = first_block(r)
    ids = [first, first + 1, jnp.minimum(first + 2, HEADS - 1)]
    for j in range(3):
        grad = part[:, pl.ds(pl.multiple_of(ids[j] * BLK, BLK), BLK)].astype(F32)
        for k in range(1, R):
            rr = (r + k) % R
            if j < 2:
                grad += m1a[rr, :, j * BLK:(j + 1) * BLK].astype(F32)
            else:
                grad += m1b[rr].astype(F32)
        turned[:, j * BLK:(j + 1) * BLK] = contract(grad.astype(BF16), bases[ids[j]], 1, 0).astype(BF16)

    halo = {
        0: [(128, 32, 0, 1)],
        1: [(0, 96, 160, 0), (96, 64, 0, 2)],
        2: [(64, 96, 0, 3), (0, 64, 192, 1)],
        3: [(0, 32, 224, 2)],
    }

    def halo_copies(me):
        out = []
        for i, (row, n, to_row, to) in enumerate(halo[me]):
            out.append(remote(
                turned.at[pl.ds(row, n)], win.at[pl.ds(to_row, n)],
                m2_s.at[i], m2_r.at[i], at(z, to // 2, to % 2, t, r),
            ))
        return out

    for me in range(4):
        @pl.when(q == me)
        def _():
            for cp in halo_copies(me):
                cp.start()

    win[pl.ds(pl.multiple_of(32 * q, 32), ROWS), :] = turned[...]

    v2 = []
    for h in range(2):
        part_h = pl.ds(h * PART, PART)
        for k in range(1, R):
            rr = (r + k) % R
            arrived(v1_recv.at[rr, part_h], v1_r.at[h, rr], v1_s.at[h, 0])
        for j in range(h * PART, (h + 1) * PART):
            acc = v1_buf[r, j].astype(F32)
            for k in range(1, R):
                acc += v1_recv[(r + k) % R, j].astype(F32)
            v2_send[j] = acc.astype(BF16)
        for p in range(h * PART // 2, (h + 1) * PART // 2):
            if PAIRS[p]:
                v2.append(remote(
                    v2_send.at[pl.ds(2 * p, 2)], v2_recv.at[z],
                    v2_s.at[p], v2_r.at[z], at((z + PAIRS[p]) % Z, yh, c, t, r),
                ))
                v2[-1].start()

    total = e2_buf[z]
    for k in range(1, Z):
        zz = (z + k) % Z
        arrived(e2_buf.at[zz], e2_r.at[zz], e2_s.at[0])
        total += e2_buf[zz]
    e3_send[...] = total
    out_rows = pl.ds(pl.multiple_of(8 * half, 8), 8)

    def share_in(k):
        y_to, c_to = (yh + k // 2) % 2, k % 2
        return remote(e3_send, ei_buf.at[yh], ei_s.at[k], ei_r.at[yh], at(z, y_to, c_to, t, r))

    def share_out(k):
        y_to, c_to, t_to = (yh + (k // 2) % 2) % 2, (1 + k) % 2, (t + k // 4) % 4
        return remote(e3_send.at[out_rows], eo_buf.at[yh], eo_s.at[k], eo_r.at[yh], at(z, y_to, c_to, t_to, r))

    @pl.when(c == 0)
    def _():
        for k in range(1, 4):
            share_in(k).start()
        ei_buf[yh] = e3_send[...]

    @pl.when((c == 1) & (t == home_t))
    def _():
        for k in range(1, 16):
            share_out(k).start()
        eo_buf[yh] = e3_send[out_rows, :]

    def halo_arrivals(me):
        for src in range(4):
            for i, (row, n, to_row, to) in enumerate(halo[src]):
                if to == me:
                    arrived(win.at[pl.ds(to_row, n)], m2_r.at[i], m2_s.at[0])

    for me in range(4):
        @pl.when(q == me)
        def _():
            halo_arrivals(me)

    @pl.when(t == home_t)
    def _():
        pltpu.make_async_copy(qg_hbm.at[pl.ds(5 * half + q, 2)], gwin, local_sem.at[6]).wait()

    @pl.when(t != home_t)
    def _():
        arrived(gwin, g_r, g_s.at[0])

    inner = [contract(gwin[b], win[b * BLK:(b + 1) * BLK, :], 0, 0) for b in range(2)]

    @pl.when(c == 1)
    def _():
        arrived(ei_buf.at[yh], ei_r.at[yh], ei_s.at[0])

    @pl.when((c == 0) | (t != home_t))
    def _():
        arrived(eo_buf.at[yh], eo_r.at[yh], eo_s.at[0])

    arrived(ei_buf.at[1 - yh], ei_r.at[1 - yh], ei_s.at[0])
    arrived(eo_buf.at[1 - yh], eo_r.at[1 - yh], eo_s.at[0])

    eig_cols = []
    for b in range(2):
        row = pl.ds(q + b, 1)
        eig_out = eo_buf[0, row, :] + eo_buf[1, row, :]
        eig_cols.append(jnp.transpose(jnp.broadcast_to(eig_out, (BLK, BLK))))

    def block_at(j, rr):
        return pl.ds(pl.multiple_of((first_block(rr) + j) * BLK, BLK), BLK)

    def m3(j, k):
        return remote(upd.at[j], update_hbm.at[:, block_at(j, r)], m3_s.at[j, k], m3_r.at[j, r], at(z, yh, c, t, (r + k) % R))

    def own_block(j):
        return pltpu.make_async_copy(upd.at[j], update_hbm.at[:, block_at(j, r)], local_sem.at[7 + j])

    def send_block(j):
        for k in X_ORDER:
            m3(j, k).start()
        own_block(j).start()

    for j in range(3):
        cols = slice(j * BLK, (j + 1) * BLK)
        row_j = pl.ds(ids[j], 1)
        eig_in = ei_buf[0, row_j, :] + ei_buf[1, row_j, :]
        for b in range(2):
            scaled = (inner[b][:, cols] / (eig_cols[b] * eig_in + DAMPING)).astype(BF16)
            back[b * BLK:(b + 1) * BLK, :] = contract(gwin[b], scaled, 1, 0).astype(BF16)
        own_rows = back[pl.ds(pl.multiple_of(32 * q, 32), ROWS), :]
        upd[j] = contract(own_rows, bases[ids[j]], 1, 1).astype(BF16)
        if j < 2:
            send_block(j)
        else:
            pl.when(r % 2 == 0)(lambda: send_block(2))

    for k in range(1, Z):
        zz = (z + k) % Z
        arrived(v2_recv.at[zz], v2_r.at[zz], v2_s.at[0])

    def over_z(y):
        acc = v2_send[2 * (Z - 1) + y].astype(F32)
        for k in range(1, Z):
            acc += v2_recv[(z + k) % Z, y].astype(F32)
        return acc

    vy_send[...] = over_z(1 - yh).astype(BF16)
    vy = remote(vy_send, vy_recv, vy_s, vy_r, at(z, 1 - yh, c, t, r))
    vy.start()
    kept = over_z(yh)
    vy.wait_recv()
    v3_buf[r] = (kept + vy_recv[...].astype(F32)).astype(BF16)
    v3 = []
    for k in X_ORDER:
        v3.append(remote(v3_buf.at[r], v3_buf.at[r], v3_s.at[k], v3_r.at[r], at(z, yh, c, t, (r + k) % R)))
        v3[-1].start()
    for k in range(1, R):
        rr = (r + k) % R
        arrived(v3_buf.at[rr], v3_r.at[rr], v3_s.at[0])
    for i in range(R):
        old_rows = fac[i * QR:(i + 1) * QR, :]
        refreshed = DECAY * old_rows + (1.0 - DECAY) * (v3_buf[i].astype(F32) * (1.0 / TOKENS))
        fac_out[i * QR:(i + 1) * QR, :] = jnp.where(own_u > 0.0, refreshed, old_rows)

    for j in range(2):
        own_block(j).wait()
    for k in range(1, R):
        rr = (r + k) % R
        for j in range(2):
            arrived(update_hbm.at[:, block_at(j, rr)], m3_r.at[j, rr], m3_s.at[j, 0])

        @pl.when(rr % 2 == 0)
        def _():
            arrived(update_hbm.at[:, block_at(2, rr)], m3_r.at[2, rr], m3_s.at[2, 0])

    for k in range(1, R):
        m1[k - 1].wait_send()
        for j in range(2):
            m3(j, k).wait_send()

        @pl.when((r + k) % 2 == 0)
        def _():
            remote(m1b.at[0], m1b.at[0], m1b_s.at[k], m1b_r.at[0], me_dev).wait_send()

    @pl.when(r % 2 == 0)
    def _():
        for k in range(1, R):
            m3(2, k).wait_send()
        own_block(2).wait()

    @pl.when(t == home_t)
    def _():
        for k in range(1, 4):
            remote(gwin, gwin, g_s.at[k], g_r, me_dev).wait_send()

    @pl.when(c == 0)
    def _():
        for k in range(1, 4):
            share_in(k).wait_send()

    @pl.when((c == 1) & (t == home_t))
    def _():
        for k in range(1, 16):
            share_out(k).wait_send()

    for cp in v0 + e1 + e2 + v1 + v2 + [vy] + v3:
        cp.wait_send()
    for me in range(4):
        @pl.when(q == me)
        def _():
            for cp in halo_copies(me):
                cp.wait_send()


def place(update_in, fac_in, update_out, fac_new, held, held_fac, in_sem, out_sem):
    rows = ROWS // 5
    steps = [(fac_in, held_fac, fac_new)]
    for i in range(5):
        at = pl.ds(i * rows, rows)
        steps.append((update_in.at[at], held.at[at], update_out.at[at]))
    come = [pltpu.make_async_copy(src, mid, in_sem.at[i]) for i, (src, mid, _) in enumerate(steps)]
    go = [pltpu.make_async_copy(mid, dst, out_sem.at[i]) for i, (_, mid, dst) in enumerate(steps)]
    for cp in come:
        cp.start()
    for arrive, leave in zip(come, go):
        arrive.wait()
        leave.start()
    for cp in go:
        cp.wait()


def per_device(acts, out_grads, grad_parts, basis_a, basis_g, fac_old, owner_slot):
    sem = pltpu.SemaphoreType.DMA
    half_slots = SLOTS // 2
    hbm = pl.BlockSpec(memory_space=pl.ANY)
    update, fac_new = pl.pallas_call(
        kernel,
        out_shape=(
            jax.ShapeDtypeStruct((ROWS, HEADS * BLK), BF16),
            jax.ShapeDtypeStruct((BLK, BLK), F32),
        ),
        in_specs=[pl.BlockSpec(memory_space=pltpu.SMEM)] + [hbm] * 6,
        out_specs=(hbm, pl.BlockSpec(memory_space=pltpu.VMEM)),
        scratch_shapes=[
            pltpu.VMEM((256, HEADS * BLK), BF16),
            pltpu.VMEM((256, HEADS * BLK), BF16),
            pltpu.VMEM((ROWS, HEADS * BLK), BF16),
            pltpu.VMEM((FACTORS, BLK, BLK), BF16),
            pltpu.VMEM((BLK, BLK), F32),
            pltpu.VMEM((2, BLK, BLK), BF16),
            pltpu.VMEM((FACTORS, BLK, BLK), F32),
            pltpu.SMEM((SLOTS,), jnp.int32),
            pltpu.SMEM((SLOTS,), jnp.int32),
            pltpu.VMEM((half_slots, BLK, BLK), BF16),
            pltpu.VMEM((half_slots, BLK, BLK), BF16),
            pltpu.VMEM((R, half_slots, QR, BLK), BF16),
            pltpu.VMEM((R, half_slots, QR, BLK), BF16),
            pltpu.VMEM((half_slots, QR, BLK), BF16),
            pltpu.VMEM((Z, 2, QR, BLK), BF16),
            pltpu.VMEM((QR, BLK), BF16),
            pltpu.VMEM((QR, BLK), BF16),
            pltpu.VMEM((R, QR, BLK), BF16),
            pltpu.VMEM((SLOTS, BLK), F32),
            pltpu.VMEM((8, 16, BLK), F32),
            pltpu.VMEM((Z, 16, BLK), F32),
            pltpu.VMEM((16, BLK), F32),
            pltpu.VMEM((2, 16, BLK), F32),
            pltpu.VMEM((2, 8, BLK), F32),
            pltpu.VMEM((R, ROWS, 2 * BLK), BF16),
            pltpu.VMEM((R, ROWS, BLK), BF16),
            pltpu.VMEM((ROWS, 3 * BLK), BF16),
            pltpu.VMEM((WIN, 3 * BLK), BF16),
            pltpu.VMEM((WIN, BLK), BF16),
            pltpu.VMEM((3, ROWS, BLK), BF16),
            sem((10,)),
            sem((R,)), sem((R,)), sem((R,)), sem((R,)),
            sem((4,)), sem,
            sem((2,)), sem((2,)),
            sem((2, R)), sem((2, R)),
            sem((Z,)), sem((Z,)),
            sem, sem,
            sem((R,)), sem((R,)),
            sem((8,)), sem((8,)),
            sem((Z,)), sem((Z,)),
            sem((4,)), sem((2,)),
            sem((16,)), sem((2,)),
            sem((2,)), sem((2,)),
            sem((3, R)), sem((3, R)),
        ],
        compiler_params=pltpu.CompilerParams(
            collective_id=0, has_side_effects=True, vmem_limit_bytes=60 * 1024 * 1024
        ),
    )(owner_slot, acts, out_grads, grad_parts[0], basis_a, basis_g, fac_old[0, 0])
    update, fac_new = pl.pallas_call(
        place,
        out_shape=(jax.ShapeDtypeStruct(update.shape, BF16), jax.ShapeDtypeStruct(fac_new.shape, F32)),
        in_specs=[hbm, hbm],
        out_specs=(hbm, hbm),
        scratch_shapes=[pltpu.VMEM(update.shape, BF16), pltpu.VMEM(fac_new.shape, F32), sem((6,)), sem((6,))],
        compiler_params=pltpu.CompilerParams(vmem_limit_bytes=60 * 1024 * 1024),
    )(update, fac_new)
    return update, fac_new[None, None]


def solution(mesh):
    placed = (
        P(("dp", "replica"), "tensor"),
        P(("dp", "replica"), "tensor"),
        P("replica", "dp", "tensor"),
        P("tensor", None, None),
        P("tensor", None, None),
        P("tensor", "dp", None, None),
        P(),
    )
    return jax.shard_map(
        per_device,
        mesh=mesh,
        in_specs=placed,
        out_specs=(P("dp", "tensor"), P("tensor", "dp", None, None)),
        check_vma=False,
    )
```

```python
import jax
import jax.numpy as jnp
from jax import lax
from jax.experimental import pallas as pl
from jax.experimental.pallas import tpu as pltpu
from jax.sharding import PartitionSpec as P

MESH = pl.DeviceIdType.MESH
F32, BF16 = jnp.float32, jnp.bfloat16

DECAY = 0.5
DAMPING = 0.01
TOKENS = 32768
BLK = 128
HEADS = 10
FACTORS = 2 * HEADS
ROWS = 160
WIN = 2 * BLK
SLOTS = 32
Z, R = 8, 4
QR = BLK // R
X_ORDER = (2, 1, 3)
Z_ORDER = (4, 3, 5, 2, 6, 1, 7)
PAIRS = Z_ORDER + (0,)
PART = SLOTS // 4


def contract(a, b, da, db):
    return lax.dot_general(a, b, (((da,), (db,)), ((), ())), preferred_element_type=F32)


def kernel(
    owner, acts_hbm, grads_hbm, parts_hbm, qa_hbm, qg_hbm, fac_hbm,
    update_hbm, fac_out,
    acts, outg, part, bases, fac, gwin, cov, slot_f, slot_u,
    v0_send, v0_recv, v1_buf, v1_recv, v2_send, v2_recv, vy_send, vy_recv, v3_buf,
    e_part, e1_buf, e2_buf, e3_send, ei_buf, eo_buf,
    m1a, m1b, turned, win, back, upd,
    local_sem, m1a_s, m1a_r, m1b_s, m1b_r, g_s, g_r, v0_s, v0_r, v1_s, v1_r, v2_s, v2_r, vy_s, vy_r,
    v3_s, v3_r, e1_s, e1_r, e2_s, e2_r, ei_s, ei_r, eo_s, eo_r, m2_s, m2_r, m3_s, m3_r,
):
    d = lax.axis_index("dp")
    t = lax.axis_index("tensor")
    r = lax.axis_index("replica")
    z, q = d // 4, d % 4
    yh, c = q // 2, q % 2
    home_t = z // 2
    half = z % 2

    def at(zz, yy, cc, tt, rr):
        return (zz * 4 + yy * 2 + cc, tt, rr)

    me_dev = at(z, yh, c, t, r)

    def remote(src, dst, s, rcv, dev):
        return pltpu.make_async_remote_copy(
            src_ref=src, dst_ref=dst, send_sem=s, recv_sem=rcv, device_id=dev, device_id_type=MESH
        )

    def arrived(dst, rcv, s):
        remote(dst, dst, s, rcv, me_dev).wait_recv()

    def first_block(rr):
        return (5 * rr + 1) // 2

    loads = [
        pltpu.make_async_copy(acts_hbm, acts, local_sem.at[0]),
        pltpu.make_async_copy(grads_hbm, outg, local_sem.at[1]),
        pltpu.make_async_copy(qa_hbm, bases.at[pl.ds(0, HEADS)], local_sem.at[2]),
        pltpu.make_async_copy(qg_hbm, bases.at[pl.ds(HEADS, HEADS)], local_sem.at[3]),
        pltpu.make_async_copy(fac_hbm, fac, local_sem.at[4]),
        pltpu.make_async_copy(parts_hbm, part, local_sem.at[5]),
    ]
    for cp in loads:
        cp.start()

    peers = []
    for k in range(1, R):
        for j in range(2):
            peers.append(at(z, yh, (c + j) % 2, t, (r + k) % R))
    for k in range(4):
        for j in range(2):
            for i in range(2):
                if k or j or i:
                    peers.append(at(z, (yh + j) % 2, (c + i) % 2, (t + k) % 4, r))
    for k in range(1, Z):
        peers.append(at((z + k) % Z, yh, c, t, r))
    barrier = pltpu.get_barrier_semaphore()
    for dev in peers:
        pl.semaphore_signal(barrier, inc=1, device_id=dev, device_id_type=MESH)

    def lookup(s, carry):
        f, u = jnp.int32(0), jnp.int32(0)
        for k in range(FACTORS):
            hit = owner[t, k] == s
            f, u = jnp.where(hit, k, f), jnp.where(hit, 1, u)
        slot_f[s] = f
        slot_u[s] = u
        return carry

    lax.fori_loop(0, SLOTS, lookup, 0)

    for side in range(2):
        src = acts if side == 0 else outg
        loads[side].wait()
        for b in range(HEADS):
            a = src[:, b * BLK:(b + 1) * BLK]
            cov[side * HEADS + b] = contract(a, a, 0, 0)

    def pick(s):
        return cov[slot_f[s]] * slot_u[s].astype(F32)

    def slot(j, core):
        return (z + PAIRS[j // 2]) % Z * 4 + j % 2 * 2 + core

    for j in range(SLOTS // 2):
        v0_send[j] = pick(slot(j, 1 - c)).astype(BF16)

    loads[2].wait()
    loads[3].wait()
    loads[4].wait()
    e_part[...] = jnp.zeros_like(e_part)
    for f in range(FACTORS):
        src = acts if f < HEADS else outg
        b = f % HEADS
        rot = contract(src[:, b * BLK:(b + 1) * BLK], bases[f], 1, 0)
        at_row = f if f < HEADS else (f + 6 if f < 15 else f + 9)
        e_part[at_row:at_row + 1, :] = jnp.sum(rot * rot, axis=0, keepdims=True) * (DECAY / TOKENS)
    own_f = slot_f[d]
    own_u = slot_u[d].astype(F32)
    own_q = bases[own_f]
    old = fac[...]
    hi = old.astype(BF16)
    rest = old - hi.astype(F32)
    mid = rest.astype(BF16)
    low = (rest - mid.astype(F32)).astype(BF16)
    fq = contract(hi, own_q, 1, 0) + contract(mid, own_q, 1, 0) + contract(low, own_q, 1, 0)
    diag = jnp.sum(own_q.astype(F32) * fq, axis=0, keepdims=True)
    place = own_f + jnp.where(own_f >= 10, 6, 0) + jnp.where(own_f >= 15, 3, 0)
    share = DECAY * own_u * (r == 0).astype(F32)
    rows = lax.broadcasted_iota(jnp.int32, (SLOTS, BLK), 0)
    e_part[...] += jnp.where(rows == place, diag * share, 0.0)

    pl.semaphore_wait(barrier, len(peers))

    v0 = []
    for h in range(2):
        part_h = pl.ds(h * PART, PART)
        v0.append(remote(v0_send.at[part_h], v0_recv.at[part_h], v0_s.at[h], v0_r.at[h], at(z, yh, 1 - c, t, r)))
        v0[-1].start()

    e1 = []
    own8 = 2 * r + c
    for k in range(1, 8):
        to = (own8 + k) % 8
        rows_to = pl.ds(pl.multiple_of(16 * (to % 2), 16), 16)
        e1.append(remote(e_part.at[rows_to], e1_buf.at[own8], e1_s.at[k], e1_r.at[own8], at(z, yh, to % 2, t, to // 2)))
        e1[-1].start()

    m1 = []
    for k in range(1, R):
        rr = (r + k) % R
        first = pl.multiple_of(first_block(rr) * BLK, BLK)
        m1.append(remote(parts_hbm.at[:, pl.ds(first, 2 * BLK)], m1a.at[r], m1a_s.at[k], m1a_r.at[r], at(z, yh, c, t, rr)))
        m1[-1].start()

        @pl.when(rr % 2 == 0)
        def _():
            third = pl.multiple_of((first_block(rr) + 2) * BLK, BLK)
            remote(parts_hbm.at[:, pl.ds(third, BLK)], m1b.at[r], m1b_s.at[k], m1b_r.at[r], at(z, yh, c, t, rr)).start()

    @pl.when(t == home_t)
    def _():
        for k in range(1, 4):
            remote(qg_hbm.at[pl.ds(5 * half + q, 2)], gwin, g_s.at[k], g_r, at(z, yh, c, (t + k) % 4, r)).start()
        pltpu.make_async_copy(qg_hbm.at[pl.ds(5 * half + q, 2)], gwin, local_sem.at[6]).start()

    v1 = []
    for h in range(2):
        v0[h].wait_recv()
        for j in range(h * PART, (h + 1) * PART):
            both = (pick(slot(j, c)) + v0_recv[j].astype(F32)).astype(BF16)
            for i in range(R):
                v1_buf[i, j] = both[i * QR:(i + 1) * QR]
        part_h = pl.ds(h * PART, PART)
        for k in X_ORDER:
            rr = (r + k) % R
            v1.append(remote(
                v1_buf.at[rr, part_h], v1_recv.at[r, part_h],
                v1_s.at[h, k], v1_r.at[h, r], at(z, yh, c, t, rr),
            ))
            v1[-1].start()

    total = e_part[pl.ds(pl.multiple_of(16 * c, 16), 16), :]
    for k in range(1, 8):
        frm = (own8 + k) % 8
        arrived(e1_buf.at[frm], e1_r.at[frm], e1_s.at[0])
        total += e1_buf[frm]
    e2_buf[z] = total
    e2 = []
    for k in Z_ORDER:
        e2.append(remote(e2_buf.at[z], e2_buf.at[z], e2_s.at[k], e2_r.at[z], at((z + k) % Z, yh, c, t, r)))
        e2[-1].start()

    loads[5].wait()
    for k in range(1, R):
        rr = (r + k) % R
        arrived(m1a.at[rr], m1a_r.at[rr], m1a_s.at[0])

        @pl.when(r % 2 == 0)
        def _():
            arrived(m1b.at[rr], m1b_r.at[rr], m1b_s.at[0])

    first = first_block(r)
    ids = [first, first + 1, jnp.minimum(first + 2, HEADS - 1)]
    for j in range(3):
        grad = part[:, pl.ds(pl.multiple_of(ids[j] * BLK, BLK), BLK)].astype(F32)
        for k in range(1, R):
            rr = (r + k) % R
            if j < 2:
                grad += m1a[rr, :, j * BLK:(j + 1) * BLK].astype(F32)
            else:
                grad += m1b[rr].astype(F32)
        turned[:, j * BLK:(j + 1) * BLK] = contract(grad.astype(BF16), bases[ids[j]], 1, 0).astype(BF16)

    halo = {
        0: [(128, 32, 0, 1)],
        1: [(0, 96, 160, 0), (96, 64, 0, 2)],
        2: [(64, 96, 0, 3), (0, 64, 192, 1)],
        3: [(0, 32, 224, 2)],
    }

    def halo_copies(me):
        out = []
        for i, (row, n, to_row, to) in enumerate(halo[me]):
            out.append(remote(
                turned.at[pl.ds(row, n)], win.at[pl.ds(to_row, n)],
                m2_s.at[i], m2_r.at[i], at(z, to // 2, to % 2, t, r),
            ))
        return out

    for me in range(4):
        @pl.when(q == me)
        def _():
            for cp in halo_copies(me):
                cp.start()

    win[pl.ds(pl.multiple_of(32 * q, 32), ROWS), :] = turned[...]

    total = e2_buf[z]
    for k in range(1, Z):
        zz = (z + k) % Z
        arrived(e2_buf.at[zz], e2_r.at[zz], e2_s.at[0])
        total += e2_buf[zz]
    e3_send[...] = total
    out_rows = pl.ds(pl.multiple_of(8 * half, 8), 8)

    def share_in(k):
        y_to, c_to = (yh + k // 2) % 2, k % 2
        return remote(e3_send, ei_buf.at[yh], ei_s.at[k], ei_r.at[yh], at(z, y_to, c_to, t, r))

    def share_out(k):
        y_to, c_to, t_to = (yh + (k // 2) % 2) % 2, (1 + k) % 2, (t + k // 4) % 4
        return remote(e3_send.at[out_rows], eo_buf.at[yh], eo_s.at[k], eo_r.at[yh], at(z, y_to, c_to, t_to, r))

    @pl.when(c == 0)
    def _():
        for k in range(1, 4):
            share_in(k).start()
        ei_buf[yh] = e3_send[...]

    @pl.when((c == 1) & (t == home_t))
    def _():
        for k in range(1, 16):
            share_out(k).start()
        eo_buf[yh] = e3_send[out_rows, :]

    v2 = []
    for h in range(2):
        part_h = pl.ds(h * PART, PART)
        for k in range(1, R):
            rr = (r + k) % R
            arrived(v1_recv.at[rr, part_h], v1_r.at[h, rr], v1_s.at[h, 0])
        for j in range(h * PART, (h + 1) * PART):
            acc = v1_buf[r, j].astype(F32)
            for k in range(1, R):
                acc += v1_recv[(r + k) % R, j].astype(F32)
            v2_send[j] = acc.astype(BF16)
        for p in range(h * PART // 2, (h + 1) * PART // 2):
            if PAIRS[p]:
                v2.append(remote(
                    v2_send.at[pl.ds(2 * p, 2)], v2_recv.at[z],
                    v2_s.at[p], v2_r.at[z], at((z + PAIRS[p]) % Z, yh, c, t, r),
                ))
                v2[-1].start()

    def halo_arrivals(me):
        for src in range(4):
            for i, (row, n, to_row, to) in enumerate(halo[src]):
                if to == me:
                    arrived(win.at[pl.ds(to_row, n)], m2_r.at[i], m2_s.at[0])

    for me in range(4):
        @pl.when(q == me)
        def _():
            halo_arrivals(me)

    @pl.when(t == home_t)
    def _():
        pltpu.make_async_copy(qg_hbm.at[pl.ds(5 * half + q, 2)], gwin, local_sem.at[6]).wait()

    @pl.when(t != home_t)
    def _():
        arrived(gwin, g_r, g_s.at[0])

    inner = [contract(gwin[b], win[b * BLK:(b + 1) * BLK, :], 0, 0) for b in range(2)]

    @pl.when(c == 1)
    def _():
        arrived(ei_buf.at[yh], ei_r.at[yh], ei_s.at[0])

    @pl.when((c == 0) | (t != home_t))
    def _():
        arrived(eo_buf.at[yh], eo_r.at[yh], eo_s.at[0])

    arrived(ei_buf.at[1 - yh], ei_r.at[1 - yh], ei_s.at[0])
    arrived(eo_buf.at[1 - yh], eo_r.at[1 - yh], eo_s.at[0])

    eig_cols = []
    for b in range(2):
        row = pl.ds(q + b, 1)
        eig_out = eo_buf[0, row, :] + eo_buf[1, row, :]
        eig_cols.append(jnp.transpose(jnp.broadcast_to(eig_out, (BLK, BLK))))

    def block_at(j, rr):
        return pl.ds(pl.multiple_of((first_block(rr) + j) * BLK, BLK), BLK)

    def m3(j, k):
        return remote(upd.at[j], update_hbm.at[:, block_at(j, r)], m3_s.at[j, k], m3_r.at[j, r], at(z, yh, c, t, (r + k) % R))

    def own_block(j):
        return pltpu.make_async_copy(upd.at[j], update_hbm.at[:, block_at(j, r)], local_sem.at[7 + j])

    def send_block(j):
        for k in X_ORDER:
            m3(j, k).start()
        own_block(j).start()

    for j in range(3):
        cols = slice(j * BLK, (j + 1) * BLK)
        row_j = pl.ds(ids[j], 1)
        eig_in = ei_buf[0, row_j, :] + ei_buf[1, row_j, :]
        for b in range(2):
            scaled = (inner[b][:, cols] / (eig_cols[b] * eig_in + DAMPING)).astype(BF16)
            back[b * BLK:(b + 1) * BLK, :] = contract(gwin[b], scaled, 1, 0).astype(BF16)
        own_rows = back[pl.ds(pl.multiple_of(32 * q, 32), ROWS), :]
        upd[j] = contract(own_rows, bases[ids[j]], 1, 1).astype(BF16)
        if j < 2:
            send_block(j)
        else:
            pl.when(r % 2 == 0)(lambda: send_block(2))

    for k in range(1, Z):
        zz = (z + k) % Z
        arrived(v2_recv.at[zz], v2_r.at[zz], v2_s.at[0])

    def over_z(y):
        acc = v2_send[2 * (Z - 1) + y].astype(F32)
        for k in range(1, Z):
            acc += v2_recv[(z + k) % Z, y].astype(F32)
        return acc

    vy_send[...] = over_z(1 - yh).astype(BF16)
    vy = remote(vy_send, vy_recv, vy_s, vy_r, at(z, 1 - yh, c, t, r))
    vy.start()
    kept = over_z(yh)
    vy.wait_recv()
    v3_buf[r] = (kept + vy_recv[...].astype(F32)).astype(BF16)
    v3 = []
    for k in X_ORDER:
        v3.append(remote(v3_buf.at[r], v3_buf.at[r], v3_s.at[k], v3_r.at[r], at(z, yh, c, t, (r + k) % R)))
        v3[-1].start()
    for k in range(1, R):
        rr = (r + k) % R
        arrived(v3_buf.at[rr], v3_r.at[rr], v3_s.at[0])
    for i in range(R):
        old_rows = fac[i * QR:(i + 1) * QR, :]
        refreshed = DECAY * old_rows + (1.0 - DECAY) * (v3_buf[i].astype(F32) * (1.0 / TOKENS))
        fac_out[i * QR:(i + 1) * QR, :] = jnp.where(own_u > 0.0, refreshed, old_rows)

    for j in range(2):
        own_block(j).wait()
    for k in range(1, R):
        rr = (r + k) % R
        for j in range(2):
            arrived(update_hbm.at[:, block_at(j, rr)], m3_r.at[j, rr], m3_s.at[j, 0])

        @pl.when(rr % 2 == 0)
        def _():
            arrived(update_hbm.at[:, block_at(2, rr)], m3_r.at[2, rr], m3_s.at[2, 0])

    for k in range(1, R):
        m1[k - 1].wait_send()
        for j in range(2):
            m3(j, k).wait_send()

        @pl.when((r + k) % 2 == 0)
        def _():
            remote(m1b.at[0], m1b.at[0], m1b_s.at[k], m1b_r.at[0], me_dev).wait_send()

    @pl.when(r % 2 == 0)
    def _():
        for k in range(1, R):
            m3(2, k).wait_send()
        own_block(2).wait()

    @pl.when(t == home_t)
    def _():
        for k in range(1, 4):
            remote(gwin, gwin, g_s.at[k], g_r, me_dev).wait_send()

    @pl.when(c == 0)
    def _():
        for k in range(1, 4):
            share_in(k).wait_send()

    @pl.when((c == 1) & (t == home_t))
    def _():
        for k in range(1, 16):
            share_out(k).wait_send()

    for cp in v0 + e1 + e2 + v1 + v2 + [vy] + v3:
        cp.wait_send()
    for me in range(4):
        @pl.when(q == me)
        def _():
            for cp in halo_copies(me):
                cp.wait_send()


def place(update_in, fac_in, update_out, fac_new, held, held_fac, in_sem, out_sem):
    rows = ROWS // 5
    steps = [(fac_in, held_fac, fac_new)]
    for i in range(5):
        at = pl.ds(i * rows, rows)
        steps.append((update_in.at[at], held.at[at], update_out.at[at]))
    come = [pltpu.make_async_copy(src, mid, in_sem.at[i]) for i, (src, mid, _) in enumerate(steps)]
    go = [pltpu.make_async_copy(mid, dst, out_sem.at[i]) for i, (_, mid, dst) in enumerate(steps)]
    for cp in come:
        cp.start()
    for arrive, leave in zip(come, go):
        arrive.wait()
        leave.start()
    for cp in go:
        cp.wait()


def per_device(acts, out_grads, grad_parts, basis_a, basis_g, fac_old, owner_slot):
    sem = pltpu.SemaphoreType.DMA
    half_slots = SLOTS // 2
    hbm = pl.BlockSpec(memory_space=pl.ANY)
    update, fac_new = pl.pallas_call(
        kernel,
        out_shape=(
            jax.ShapeDtypeStruct((ROWS, HEADS * BLK), BF16),
            jax.ShapeDtypeStruct((BLK, BLK), F32),
        ),
        in_specs=[pl.BlockSpec(memory_space=pltpu.SMEM)] + [hbm] * 6,
        out_specs=(hbm, pl.BlockSpec(memory_space=pltpu.VMEM)),
        scratch_shapes=[
            pltpu.VMEM((256, HEADS * BLK), BF16),
            pltpu.VMEM((256, HEADS * BLK), BF16),
            pltpu.VMEM((ROWS, HEADS * BLK), BF16),
            pltpu.VMEM((FACTORS, BLK, BLK), BF16),
            pltpu.VMEM((BLK, BLK), F32),
            pltpu.VMEM((2, BLK, BLK), BF16),
            pltpu.VMEM((FACTORS, BLK, BLK), F32),
            pltpu.SMEM((SLOTS,), jnp.int32),
            pltpu.SMEM((SLOTS,), jnp.int32),
            pltpu.VMEM((half_slots, BLK, BLK), BF16),
            pltpu.VMEM((half_slots, BLK, BLK), BF16),
            pltpu.VMEM((R, half_slots, QR, BLK), BF16),
            pltpu.VMEM((R, half_slots, QR, BLK), BF16),
            pltpu.VMEM((half_slots, QR, BLK), BF16),
            pltpu.VMEM((Z, 2, QR, BLK), BF16),
            pltpu.VMEM((QR, BLK), BF16),
            pltpu.VMEM((QR, BLK), BF16),
            pltpu.VMEM((R, QR, BLK), BF16),
            pltpu.VMEM((SLOTS, BLK), F32),
            pltpu.VMEM((8, 16, BLK), F32),
            pltpu.VMEM((Z, 16, BLK), F32),
            pltpu.VMEM((16, BLK), F32),
            pltpu.VMEM((2, 16, BLK), F32),
            pltpu.VMEM((2, 8, BLK), F32),
            pltpu.VMEM((R, ROWS, 2 * BLK), BF16),
            pltpu.VMEM((R, ROWS, BLK), BF16),
            pltpu.VMEM((ROWS, 3 * BLK), BF16),
            pltpu.VMEM((WIN, 3 * BLK), BF16),
            pltpu.VMEM((WIN, BLK), BF16),
            pltpu.VMEM((3, ROWS, BLK), BF16),
            sem((10,)),
            sem((R,)), sem((R,)), sem((R,)), sem((R,)),
            sem((4,)), sem,
            sem((2,)), sem((2,)),
            sem((2, R)), sem((2, R)),
            sem((Z,)), sem((Z,)),
            sem, sem,
            sem((R,)), sem((R,)),
            sem((8,)), sem((8,)),
            sem((Z,)), sem((Z,)),
            sem((4,)), sem((2,)),
            sem((16,)), sem((2,)),
            sem((2,)), sem((2,)),
            sem((3, R)), sem((3, R)),
        ],
        compiler_params=pltpu.CompilerParams(
            collective_id=0, has_side_effects=True, vmem_limit_bytes=60 * 1024 * 1024
        ),
    )(owner_slot, acts, out_grads, grad_parts[0], basis_a, basis_g, fac_old[0, 0])
    update, fac_new = pl.pallas_call(
        place,
        out_shape=(jax.ShapeDtypeStruct(update.shape, BF16), jax.ShapeDtypeStruct(fac_new.shape, F32)),
        in_specs=[hbm, hbm],
        out_specs=(hbm, hbm),
        scratch_shapes=[pltpu.VMEM(update.shape, BF16), pltpu.VMEM(fac_new.shape, F32), sem((6,)), sem((6,))],
        compiler_params=pltpu.CompilerParams(vmem_limit_bytes=60 * 1024 * 1024),
    )(update, fac_new)
    return update, fac_new[None, None]


def solution(mesh):
    placed = (
        P(("dp", "replica"), "tensor"),
        P(("dp", "replica"), "tensor"),
        P("replica", "dp", "tensor"),
        P("tensor", None, None),
        P("tensor", None, None),
        P("tensor", "dp", None, None),
        P(),
    )
    return jax.shard_map(
        per_device,
        mesh=mesh,
        in_specs=placed,
        out_specs=(P("dp", "tensor"), P("tensor", "dp", None, None)),
        check_vma=False,
    )
```

```python
import jax
import jax.numpy as jnp
from jax import lax
from jax.experimental import pallas as pl
from jax.experimental.pallas import tpu as pltpu
from jax.sharding import PartitionSpec as P

MESH = pl.DeviceIdType.MESH
F32, BF16 = jnp.float32, jnp.bfloat16

DECAY = 0.5
DAMPING = 0.01
TOKENS = 32768
BLK = 128
HEADS = 10
FACTORS = 2 * HEADS
ROWS = 160
WIN = 2 * BLK
SLOTS = 32
Z, R = 8, 4
QR = BLK // R
X_ORDER = (2, 1, 3)
Z_ORDER = (4, 3, 5, 2, 6, 1, 7)
PAIRS = Z_ORDER + (0,)
PART = SLOTS // 4


def contract(a, b, da, db):
    return lax.dot_general(a, b, (((da,), (db,)), ((), ())), preferred_element_type=F32)


def kernel(
    owner, acts_hbm, grads_hbm, parts_hbm, qa_hbm, qg_hbm, fac_hbm,
    update_hbm, fac_out,
    acts, outg, part, bases, fac, gwin, cov, slot_f, slot_u,
    v0_send, v0_recv, v1_buf, v1_recv, v2_send, v2_recv, vy_send, vy_recv, v3_buf,
    e_part, e1_buf, e2_buf, e3_send, ei_buf, eo_buf,
    m1a, m1b, turned, win, back, upd,
    local_sem, m1a_s, m1a_r, m1b_s, m1b_r, g_s, g_r, v0_s, v0_r, v1_s, v1_r, v2_s, v2_r, vy_s, vy_r,
    v3_s, v3_r, e1_s, e1_r, e2_s, e2_r, ei_s, ei_r, eo_s, eo_r, m2_s, m2_r, m3_s, m3_r,
):
    d = lax.axis_index("dp")
    t = lax.axis_index("tensor")
    r = lax.axis_index("replica")
    z, q = d // 4, d % 4
    yh, c = q // 2, q % 2
    home_t = z // 2
    half = z % 2

    def at(zz, yy, cc, tt, rr):
        return (zz * 4 + yy * 2 + cc, tt, rr)

    me_dev = at(z, yh, c, t, r)

    def remote(src, dst, s, rcv, dev):
        return pltpu.make_async_remote_copy(
            src_ref=src, dst_ref=dst, send_sem=s, recv_sem=rcv, device_id=dev, device_id_type=MESH
        )

    def arrived(dst, rcv, s):
        remote(dst, dst, s, rcv, me_dev).wait_recv()

    def first_block(rr):
        return (5 * rr + 1) // 2

    peers = []
    for k in X_ORDER:
        for j in range(2):
            peers.append(at(z, yh, (c + j) % 2, t, (r + k) % R))
    for k in range(4):
        for j in range(2):
            for i in range(2):
                if k or j or i:
                    peers.append(at(z, (yh + j) % 2, (c + i) % 2, (t + k) % 4, r))
    for k in range(1, Z):
        peers.append(at((z + k) % Z, yh, c, t, r))
    barrier = pltpu.get_barrier_semaphore()
    for dev in peers:
        pl.semaphore_signal(barrier, inc=1, device_id=dev, device_id_type=MESH)

    loads = [
        pltpu.make_async_copy(acts_hbm, acts, local_sem.at[0]),
        pltpu.make_async_copy(grads_hbm, outg, local_sem.at[1]),
        pltpu.make_async_copy(qa_hbm, bases.at[pl.ds(0, HEADS)], local_sem.at[2]),
        pltpu.make_async_copy(qg_hbm, bases.at[pl.ds(HEADS, HEADS)], local_sem.at[3]),
        pltpu.make_async_copy(fac_hbm, fac, local_sem.at[4]),
        pltpu.make_async_copy(parts_hbm, part, local_sem.at[5]),
    ]
    for cp in loads:
        cp.start()

    def lookup(s, carry):
        f, u = jnp.int32(0), jnp.int32(0)
        for k in range(FACTORS):
            hit = owner[t, k] == s
            f, u = jnp.where(hit, k, f), jnp.where(hit, 1, u)
        slot_f[s] = f
        slot_u[s] = u
        return carry

    lax.fori_loop(0, SLOTS, lookup, 0)

    for side in range(2):
        src = acts if side == 0 else outg
        loads[side].wait()
        for b in range(HEADS):
            a = src[:, b * BLK:(b + 1) * BLK]
            cov[side * HEADS + b] = contract(a, a, 0, 0)

    def pick(s):
        return cov[slot_f[s]] * slot_u[s].astype(F32)

    def slot(j, core):
        return (z + PAIRS[j // 2]) % Z * 4 + j % 2 * 2 + core

    for j in range(SLOTS // 2):
        v0_send[j] = pick(slot(j, 1 - c)).astype(BF16)

    loads[2].wait()
    loads[3].wait()
    loads[4].wait()
    e_part[...] = jnp.zeros_like(e_part)
    for f in range(FACTORS):
        src = acts if f < HEADS else outg
        b = f % HEADS
        rot = contract(src[:, b * BLK:(b + 1) * BLK], bases[f], 1, 0)
        at_row = f if f < HEADS else (f + 6 if f < 15 else f + 9)
        e_part[at_row:at_row + 1, :] = jnp.sum(rot * rot, axis=0, keepdims=True) * (DECAY / TOKENS)
    own_f = slot_f[d]
    own_u = slot_u[d].astype(F32)
    own_q = bases[own_f]
    old = fac[...]
    hi = old.astype(BF16)
    rest = old - hi.astype(F32)
    mid = rest.astype(BF16)
    low = (rest - mid.astype(F32)).astype(BF16)
    fq = contract(hi, own_q, 1, 0) + contract(mid, own_q, 1, 0) + contract(low, own_q, 1, 0)
    diag = jnp.sum(own_q.astype(F32) * fq, axis=0, keepdims=True)
    place = own_f + jnp.where(own_f >= 10, 6, 0) + jnp.where(own_f >= 15, 3, 0)
    share = DECAY * own_u * (r == 0).astype(F32)
    rows = lax.broadcasted_iota(jnp.int32, (SLOTS, BLK), 0)
    e_part[...] += jnp.where(rows == place, diag * share, 0.0)

    pl.semaphore_wait(barrier, len(peers))

    e1 = []
    own8 = 2 * r + c
    for k in range(1, 8):
        to = (own8 + k) % 8
        rows_to = pl.ds(pl.multiple_of(16 * (to % 2), 16), 16)
        e1.append(remote(e_part.at[rows_to], e1_buf.at[own8], e1_s.at[k], e1_r.at[own8], at(z, yh, to % 2, t, to // 2)))
        e1[-1].start()

    v0 = []
    for h in range(2):
        part_h = pl.ds(h * PART, PART)
        v0.append(remote(v0_send.at[part_h], v0_recv.at[part_h], v0_s.at[h], v0_r.at[h], at(z, yh, 1 - c, t, r)))
        v0[-1].start()

    m1 = []
    for k in range(1, R):
        rr = (r + k) % R
        first = pl.multiple_of(first_block(rr) * BLK, BLK)
        m1.append(remote(parts_hbm.at[:, pl.ds(first, 2 * BLK)], m1a.at[r], m1a_s.at[k], m1a_r.at[r], at(z, yh, c, t, rr)))
        m1[-1].start()

        @pl.when(rr % 2 == 0)
        def _():
            third = pl.multiple_of((first_block(rr) + 2) * BLK, BLK)
            remote(parts_hbm.at[:, pl.ds(third, BLK)], m1b.at[r], m1b_s.at[k], m1b_r.at[r], at(z, yh, c, t, rr)).start()

    v1 = []
    for h in range(2):
        v0[h].wait_recv()
        for j in range(h * PART, (h + 1) * PART):
            both = (pick(slot(j, c)) + v0_recv[j].astype(F32)).astype(BF16)
            for i in range(R):
                v1_buf[i, j] = both[i * QR:(i + 1) * QR]
        part_h = pl.ds(h * PART, PART)
        for k in X_ORDER:
            rr = (r + k) % R
            v1.append(remote(
                v1_buf.at[rr, part_h], v1_recv.at[r, part_h],
                v1_s.at[h, k], v1_r.at[h, r], at(z, yh, c, t, rr),
            ))
            v1[-1].start()

    @pl.when(t == home_t)
    def _():
        for k in range(1, 4):
            remote(qg_hbm.at[pl.ds(5 * half + q, 2)], gwin, g_s.at[k], g_r, at(z, yh, c, (t + k) % 4, r)).start()
        pltpu.make_async_copy(qg_hbm.at[pl.ds(5 * half + q, 2)], gwin, local_sem.at[6]).start()

    total = e_part[pl.ds(pl.multiple_of(16 * c, 16), 16), :]
    for k in range(1, 8):
        frm = (own8 + k) % 8
        arrived(e1_buf.at[frm], e1_r.at[frm], e1_s.at[0])
        total += e1_buf[frm]
    e2_buf[z] = total
    e2 = []
    for k in Z_ORDER:
        e2.append(remote(e2_buf.at[z], e2_buf.at[z], e2_s.at[k], e2_r.at[z], at((z + k) % Z, yh, c, t, r)))
        e2[-1].start()

    total = e2_buf[z]
    for k in range(1, Z):
        zz = (z + k) % Z
        arrived(e2_buf.at[zz], e2_r.at[zz], e2_s.at[0])
        total += e2_buf[zz]
    e3_send[...] = total
    out_rows = pl.ds(pl.multiple_of(8 * half, 8), 8)

    def share_in(k):
        y_to, c_to = (yh + k // 2) % 2, k % 2
        return remote(e3_send, ei_buf.at[yh], ei_s.at[k], ei_r.at[yh], at(z, y_to, c_to, t, r))

    def share_out(k):
        y_to, c_to, t_to = (yh + (k // 2) % 2) % 2, (1 + k) % 2, (t + k // 4) % 4
        return remote(e3_send.at[out_rows], eo_buf.at[yh], eo_s.at[k], eo_r.at[yh], at(z, y_to, c_to, t_to, r))

    @pl.when(c == 0)
    def _():
        for k in range(1, 4):
            share_in(k).start()
        ei_buf[yh] = e3_send[...]

    @pl.when((c == 1) & (t == home_t))
    def _():
        for k in range(1, 16):
            share_out(k).start()
        eo_buf[yh] = e3_send[out_rows, :]

    loads[5].wait()
    for k in range(1, R):
        rr = (r + k) % R
        arrived(m1a.at[rr], m1a_r.at[rr], m1a_s.at[0])

        @pl.when(r % 2 == 0)
        def _():
            arrived(m1b.at[rr], m1b_r.at[rr], m1b_s.at[0])

    first = first_block(r)
    ids = [first, first + 1, jnp.minimum(first + 2, HEADS - 1)]
    for j in range(3):
        grad = part[:, pl.ds(pl.multiple_of(ids[j] * BLK, BLK), BLK)].astype(F32)
        for k in range(1, R):
            rr = (r + k) % R
            if j < 2:
                grad += m1a[rr, :, j * BLK:(j + 1) * BLK].astype(F32)
            else:
                grad += m1b[rr].astype(F32)
        turned[:, j * BLK:(j + 1) * BLK] = contract(grad.astype(BF16), bases[ids[j]], 1, 0).astype(BF16)

    halo = {
        0: [(128, 32, 0, 1)],
        1: [(0, 96, 160, 0), (96, 64, 0, 2)],
        2: [(64, 96, 0, 3), (0, 64, 192, 1)],
        3: [(0, 32, 224, 2)],
    }

    def halo_copies(me):
        out = []
        for i, (row, n, to_row, to) in enumerate(halo[me]):
            out.append(remote(
                turned.at[pl.ds(row, n)], win.at[pl.ds(to_row, n)],
                m2_s.at[i], m2_r.at[i], at(z, to // 2, to % 2, t, r),
            ))
        return out

    for me in range(4):
        @pl.when(q == me)
        def _():
            for cp in halo_copies(me):
                cp.start()

    win[pl.ds(pl.multiple_of(32 * q, 32), ROWS), :] = turned[...]

    v2 = []
    for h in range(2):
        part_h = pl.ds(h * PART, PART)
        for k in range(1, R):
            rr = (r + k) % R
            arrived(v1_recv.at[rr, part_h], v1_r.at[h, rr], v1_s.at[h, 0])
        for j in range(h * PART, (h + 1) * PART):
            acc = v1_buf[r, j].astype(F32)
            for k in range(1, R):
                acc += v1_recv[(r + k) % R, j].astype(F32)
            v2_send[j] = acc.astype(BF16)
        for p in range(h * PART // 2, (h + 1) * PART // 2):
            if PAIRS[p]:
                v2.append(remote(
                    v2_send.at[pl.ds(2 * p, 2)], v2_recv.at[z],
                    v2_s.at[p], v2_r.at[z], at((z + PAIRS[p]) % Z, yh, c, t, r),
                ))
                v2[-1].start()

    def halo_arrivals(me):
        for src in range(4):
            for i, (row, n, to_row, to) in enumerate(halo[src]):
                if to == me:
                    arrived(win.at[pl.ds(to_row, n)], m2_r.at[i], m2_s.at[0])

    for me in range(4):
        @pl.when(q == me)
        def _():
            halo_arrivals(me)

    @pl.when(t == home_t)
    def _():
        pltpu.make_async_copy(qg_hbm.at[pl.ds(5 * half + q, 2)], gwin, local_sem.at[6]).wait()

    @pl.when(t != home_t)
    def _():
        arrived(gwin, g_r, g_s.at[0])

    inner = [contract(gwin[b], win[b * BLK:(b + 1) * BLK, :], 0, 0) for b in range(2)]

    @pl.when(c == 1)
    def _():
        arrived(ei_buf.at[yh], ei_r.at[yh], ei_s.at[0])

    @pl.when((c == 0) | (t != home_t))
    def _():
        arrived(eo_buf.at[yh], eo_r.at[yh], eo_s.at[0])

    arrived(ei_buf.at[1 - yh], ei_r.at[1 - yh], ei_s.at[0])
    arrived(eo_buf.at[1 - yh], eo_r.at[1 - yh], eo_s.at[0])

    eig_cols = []
    for b in range(2):
        row = pl.ds(q + b, 1)
        eig_out = eo_buf[0, row, :] + eo_buf[1, row, :]
        eig_cols.append(jnp.transpose(jnp.broadcast_to(eig_out, (BLK, BLK))))

    def block_at(j, rr):
        return pl.ds(pl.multiple_of((first_block(rr) + j) * BLK, BLK), BLK)

    def m3(j, k):
        return remote(upd.at[j], update_hbm.at[:, block_at(j, r)], m3_s.at[j, k], m3_r.at[j, r], at(z, yh, c, t, (r + k) % R))

    def own_block(j):
        return pltpu.make_async_copy(upd.at[j], update_hbm.at[:, block_at(j, r)], local_sem.at[7 + j])

    def send_block(j):
        for k in X_ORDER:
            m3(j, k).start()
        own_block(j).start()

    for j in range(3):
        cols = slice(j * BLK, (j + 1) * BLK)
        row_j = pl.ds(ids[j], 1)
        eig_in = ei_buf[0, row_j, :] + ei_buf[1, row_j, :]
        for b in range(2):
            scaled = (inner[b][:, cols] / (eig_cols[b] * eig_in + DAMPING)).astype(BF16)
            back[b * BLK:(b + 1) * BLK, :] = contract(gwin[b], scaled, 1, 0).astype(BF16)
        own_rows = back[pl.ds(pl.multiple_of(32 * q, 32), ROWS), :]
        upd[j] = contract(own_rows, bases[ids[j]], 1, 1).astype(BF16)
        if j < 2:
            send_block(j)
        else:
            pl.when(r % 2 == 0)(lambda: send_block(2))

    for k in range(1, Z):
        zz = (z + k) % Z
        arrived(v2_recv.at[zz], v2_r.at[zz], v2_s.at[0])

    def over_z(y):
        acc = v2_send[2 * (Z - 1) + y].astype(F32)
        for k in range(1, Z):
            acc += v2_recv[(z + k) % Z, y].astype(F32)
        return acc

    vy_send[...] = over_z(1 - yh).astype(BF16)
    vy = remote(vy_send, vy_recv, vy_s, vy_r, at(z, 1 - yh, c, t, r))
    vy.start()
    kept = over_z(yh)
    vy.wait_recv()
    v3_buf[r] = (kept + vy_recv[...].astype(F32)).astype(BF16)
    v3 = []
    for k in X_ORDER:
        v3.append(remote(v3_buf.at[r], v3_buf.at[r], v3_s.at[k], v3_r.at[r], at(z, yh, c, t, (r + k) % R)))
        v3[-1].start()
    for k in range(1, R):
        rr = (r + k) % R
        arrived(v3_buf.at[rr], v3_r.at[rr], v3_s.at[0])
    for i in range(R):
        old_rows = fac[i * QR:(i + 1) * QR, :]
        refreshed = DECAY * old_rows + (1.0 - DECAY) * (v3_buf[i].astype(F32) * (1.0 / TOKENS))
        fac_out[i * QR:(i + 1) * QR, :] = jnp.where(own_u > 0.0, refreshed, old_rows)

    for j in range(2):
        own_block(j).wait()
    for k in range(1, R):
        rr = (r + k) % R
        for j in range(2):
            arrived(update_hbm.at[:, block_at(j, rr)], m3_r.at[j, rr], m3_s.at[j, 0])

        @pl.when(rr % 2 == 0)
        def _():
            arrived(update_hbm.at[:, block_at(2, rr)], m3_r.at[2, rr], m3_s.at[2, 0])

    for k in range(1, R):
        m1[k - 1].wait_send()
        for j in range(2):
            m3(j, k).wait_send()

        @pl.when((r + k) % 2 == 0)
        def _():
            remote(m1b.at[0], m1b.at[0], m1b_s.at[k], m1b_r.at[0], me_dev).wait_send()

    @pl.when(r % 2 == 0)
    def _():
        for k in range(1, R):
            m3(2, k).wait_send()
        own_block(2).wait()

    @pl.when(t == home_t)
    def _():
        for k in range(1, 4):
            remote(gwin, gwin, g_s.at[k], g_r, me_dev).wait_send()

    @pl.when(c == 0)
    def _():
        for k in range(1, 4):
            share_in(k).wait_send()

    @pl.when((c == 1) & (t == home_t))
    def _():
        for k in range(1, 16):
            share_out(k).wait_send()

    for cp in v0 + e1 + e2 + v1 + v2 + [vy] + v3:
        cp.wait_send()
    for me in range(4):
        @pl.when(q == me)
        def _():
            for cp in halo_copies(me):
                cp.wait_send()


def place(update_in, fac_in, update_out, fac_new, held, held_fac, in_sem, out_sem):
    rows = ROWS // 5
    steps = [(fac_in, held_fac, fac_new)]
    for i in range(5):
        at = pl.ds(i * rows, rows)
        steps.append((update_in.at[at], held.at[at], update_out.at[at]))
    come = [pltpu.make_async_copy(src, mid, in_sem.at[i]) for i, (src, mid, _) in enumerate(steps)]
    go = [pltpu.make_async_copy(mid, dst, out_sem.at[i]) for i, (_, mid, dst) in enumerate(steps)]
    for cp in come:
        cp.start()
    for arrive, leave in zip(come, go):
        arrive.wait()
        leave.start()
    for cp in go:
        cp.wait()


def per_device(acts, out_grads, grad_parts, basis_a, basis_g, fac_old, owner_slot):
    sem = pltpu.SemaphoreType.DMA
    half_slots = SLOTS // 2
    hbm = pl.BlockSpec(memory_space=pl.ANY)
    update, fac_new = pl.pallas_call(
        kernel,
        out_shape=(
            jax.ShapeDtypeStruct((ROWS, HEADS * BLK), BF16),
            jax.ShapeDtypeStruct((BLK, BLK), F32),
        ),
        in_specs=[pl.BlockSpec(memory_space=pltpu.SMEM)] + [hbm] * 6,
        out_specs=(hbm, pl.BlockSpec(memory_space=pltpu.VMEM)),
        scratch_shapes=[
            pltpu.VMEM((256, HEADS * BLK), BF16),
            pltpu.VMEM((256, HEADS * BLK), BF16),
            pltpu.VMEM((ROWS, HEADS * BLK), BF16),
            pltpu.VMEM((FACTORS, BLK, BLK), BF16),
            pltpu.VMEM((BLK, BLK), F32),
            pltpu.VMEM((2, BLK, BLK), BF16),
            pltpu.VMEM((FACTORS, BLK, BLK), F32),
            pltpu.SMEM((SLOTS,), jnp.int32),
            pltpu.SMEM((SLOTS,), jnp.int32),
            pltpu.VMEM((half_slots, BLK, BLK), BF16),
            pltpu.VMEM((half_slots, BLK, BLK), BF16),
            pltpu.VMEM((R, half_slots, QR, BLK), BF16),
            pltpu.VMEM((R, half_slots, QR, BLK), BF16),
            pltpu.VMEM((half_slots, QR, BLK), BF16),
            pltpu.VMEM((Z, 2, QR, BLK), BF16),
            pltpu.VMEM((QR, BLK), BF16),
            pltpu.VMEM((QR, BLK), BF16),
            pltpu.VMEM((R, QR, BLK), BF16),
            pltpu.VMEM((SLOTS, BLK), F32),
            pltpu.VMEM((8, 16, BLK), F32),
            pltpu.VMEM((Z, 16, BLK), F32),
            pltpu.VMEM((16, BLK), F32),
            pltpu.VMEM((2, 16, BLK), F32),
            pltpu.VMEM((2, 8, BLK), F32),
            pltpu.VMEM((R, ROWS, 2 * BLK), BF16),
            pltpu.VMEM((R, ROWS, BLK), BF16),
            pltpu.VMEM((ROWS, 3 * BLK), BF16),
            pltpu.VMEM((WIN, 3 * BLK), BF16),
            pltpu.VMEM((WIN, BLK), BF16),
            pltpu.VMEM((3, ROWS, BLK), BF16),
            sem((10,)),
            sem((R,)), sem((R,)), sem((R,)), sem((R,)),
            sem((4,)), sem,
            sem((2,)), sem((2,)),
            sem((2, R)), sem((2, R)),
            sem((Z,)), sem((Z,)),
            sem, sem,
            sem((R,)), sem((R,)),
            sem((8,)), sem((8,)),
            sem((Z,)), sem((Z,)),
            sem((4,)), sem((2,)),
            sem((16,)), sem((2,)),
            sem((2,)), sem((2,)),
            sem((3, R)), sem((3, R)),
        ],
        compiler_params=pltpu.CompilerParams(
            collective_id=0, has_side_effects=True, vmem_limit_bytes=60 * 1024 * 1024
        ),
    )(owner_slot, acts, out_grads, grad_parts[0], basis_a, basis_g, fac_old[0, 0])
    update, fac_new = pl.pallas_call(
        place,
        out_shape=(jax.ShapeDtypeStruct(update.shape, BF16), jax.ShapeDtypeStruct(fac_new.shape, F32)),
        in_specs=[hbm, hbm],
        out_specs=(hbm, hbm),
        scratch_shapes=[pltpu.VMEM(update.shape, BF16), pltpu.VMEM(fac_new.shape, F32), sem((6,)), sem((6,))],
        compiler_params=pltpu.CompilerParams(vmem_limit_bytes=60 * 1024 * 1024),
    )(update, fac_new)
    return update, fac_new[None, None]


def solution(mesh):
    placed = (
        P(("dp", "replica"), "tensor"),
        P(("dp", "replica"), "tensor"),
        P("replica", "dp", "tensor"),
        P("tensor", None, None),
        P("tensor", None, None),
        P("tensor", "dp", None, None),
        P(),
    )
    return jax.shard_map(
        per_device,
        mesh=mesh,
        in_specs=placed,
        out_specs=(P("dp", "tensor"), P("tensor", "dp", None, None)),
        check_vma=False,
    )
```
